256 devices in a mesh: tx: 4 (over x), ty: 4 (over y), tz: 16 (over z, core).
Axes of the slice: x: 4, y: 4, z: 8, core: 2. Of those that a mesh axis runs over, the one named last changes fastest.
Arguments:
- surface: float32 [4, 4, 16, 4, 3, 312], P('tx', 'ty', 'tz'), may hold values from -6 to 6
- synthesis: float32 [312, 169], replicated, may hold values from -0.5 to 0.5
- analysis: float32 [169, 312], replicated, may hold values from -0.3125 to 0.3125
- stiffness: float32 [169], replicated, may hold values from 0.1 to 10
- upsample: float32 [1248, 312], replicated, may hold values from -0.3125 to 0.3125
- quad_weight: float32 [1248], replicated, may hold values from 0.5 to 2
- near_pairs: int32 [4, 4, 16, 16, 3], P('tx', 'ty', 'tz'), may hold values from 0 to 26, as said below
- pair_count: int32 [4, 4, 16], P('tx', 'ty', 'tz'), may hold values from 1 to 16, as said below
Outputs:
- velocity: float32 [4, 4, 16, 4, 3, 312], P('tx', 'ty', 'tz')
The draws below stay inside these ranges and needn't reach their ends.
Inputs may be any that keep to these rules, and one draw needn't show every extreme that they name: `near_pairs`: column 0 and column 2 name cells 0 to 3; column 1 names a neighbour tile code 0 to 26 whose tile lies inside the mesh; when the code is 13 the two cells differ. `pair_count`: some tile uses all 16 slots.
All inputs are finite; a program needn't handle non-finite values.
Results may differ from the reference program's by a relative error of at most 0.0001.
Values sent between devices are 32-bit elements; how exact they have to be, the bound alone decides.
A program may use at most 64 MiB of HBM per device.

```python
import math
import jax
import jax.numpy as jnp
from jax import lax

NP = 312
NC = 169
NU = 1248
CPD = 4
PD = 16
N_TX = 4
N_TY = 4
N_TZ = 16


def draw_near_pairs(key, part):
    key = jax.random.fold_in(key, 11)
    subkeys = jax.random.split(key, 6)
    grid_shape = (N_TX, N_TY, N_TZ, PD)
    tile_x = lax.broadcasted_iota(jnp.int32, grid_shape, 0)
    tile_y = lax.broadcasted_iota(jnp.int32, grid_shape, 1)
    tile_z = lax.broadcasted_iota(jnp.int32, grid_shape, 2)
    shift_x = jnp.clip(tile_x + jax.random.randint(subkeys[0], grid_shape, -1, 2), 0, N_TX - 1) - tile_x
    shift_y = jnp.clip(tile_y + jax.random.randint(subkeys[1], grid_shape, -1, 2), 0, N_TY - 1) - tile_y
    shift_z = jnp.clip(tile_z + jax.random.randint(subkeys[2], grid_shape, -1, 2), 0, N_TZ - 1) - tile_z
    near_code = (shift_x + 1) * 9 + (shift_y + 1) * 3 + (shift_z + 1)
    own_cell = jax.random.randint(subkeys[3], grid_shape, 0, CPD)
    other_cell = jax.random.randint(subkeys[4], grid_shape, 0, CPD)
    stride = jax.random.randint(subkeys[5], grid_shape, 1, CPD)
    other_cell = jnp.where(near_code == 13, (own_cell + stride) % CPD, other_cell)
    return jnp.stack([own_cell, near_code, other_cell], axis=-1).astype(jnp.int32)


def draw_pair_count(key, part):
    key = jax.random.fold_in(key, 12)
    subkeys = jax.random.split(key, 2)
    grid_shape = (N_TX, N_TY, N_TZ)
    halving = jax.random.randint(subkeys[0], grid_shape, 0, 5)
    counts = jnp.right_shift(jnp.full(grid_shape, PD, jnp.int32), halving)
    counts = jnp.maximum(counts, 1)
    busiest = jax.random.randint(subkeys[1], (), 0, N_TX * N_TY * N_TZ)
    flat_id = (lax.broadcasted_iota(jnp.int32, grid_shape, 0) * N_TY + lax.broadcasted_iota(jnp.int32, grid_shape, 1)) * N_TZ + lax.broadcasted_iota(jnp.int32, grid_shape, 2)
    return jnp.where(flat_id == busiest, PD, counts).astype(jnp.int32)


def shard_levels(stream_key, shape, cuts, low, high):
    def one(position, shards_of):
        heights = jax.random.uniform(jax.random.fold_in(jax.random.fold_in(stream_key, 6), position), (shards_of,), jnp.float32, low / len(cuts), high / len(cuts))
        return jnp.repeat(jnp.exp(heights), shape[position] // shards_of).reshape((-1,) + (1,) * (len(shape) - position - 1))

    gain = one(*cuts[0])
    for cut in cuts[1:]:
        gain = gain * one(*cut)
    return gain


def scatter_about(rng, dims, scale, limit, cuts=(), kind=jnp.bfloat16):
    result = jax.random.normal(rng, dims, jnp.float32) * scale
    if len(cuts) > 0:
        result = shard_levels(rng, dims, cuts, -0.22, 0.18) * result
    return jnp.clip(result, min=-limit, max=limit).astype(kind)


def setup_inputs(seed: int = 0) -> dict:
    splits = jax.random.split(jax.random.key(seed), 9)
    return {
        "surface": scatter_about(splits[0], (N_TX, N_TY, N_TZ, CPD, 3, NP), 1.0, 6.0, ((0, 4), (1, 4), (2, 16)), jnp.float32),
        "synthesis": scatter_about(splits[1], (NP, NC), NC ** -0.5, 0.5, (), jnp.float32),
        "analysis": scatter_about(splits[2], (NC, NP), NP ** -0.5, 0.3125, (), jnp.float32),
        "stiffness": jnp.clip(jnp.exp(jax.random.uniform(splits[3], (NC,), jnp.float32, math.log(0.1), math.log(10.0))), 0.1, 10.0),
        "upsample": scatter_about(splits[4], (NU, NP), NP ** -0.5, 0.3125, (), jnp.float32),
        "quad_weight": jnp.clip(jnp.exp(jax.random.uniform(splits[5], (NU,), jnp.float32, math.log(0.5), math.log(2.0))), 0.5, 2.0),
        "near_pairs": draw_near_pairs(jax.random.fold_in(splits[8], 71), 0),
        "pair_count": draw_pair_count(jax.random.fold_in(splits[8], 71), 0),
    }


smooth_sq = 0.25

def stokes_velocity(targets, sources, density, quad_weight):
    blocks = 3
    block_width = sources.shape[-1] // blocks
    source_blocks = jnp.moveaxis(sources.reshape(3, blocks, block_width), 1, 0)
    density_blocks = jnp.moveaxis((density * quad_weight).reshape(3, blocks, block_width), 1, 0)

    def add_block(running, block_item):
        placed, weighted = block_item
        offset = targets[:, :, None] - placed[:, None, :]
        inverse = 1.0 / jnp.sqrt(lax.optimization_barrier(jnp.sum(offset * offset, axis=0)) + smooth_sq)
        along = lax.optimization_barrier(jnp.sum(offset * weighted[:, None, :], axis=0))
        summand = weighted[:, None, :] * inverse + offset * (along * inverse ** 3)
        return (running + lax.optimization_barrier(jnp.sum(summand, axis=2)), None)
    running = lax.scan(add_block, jnp.zeros(targets.shape, jnp.float32), (source_blocks, density_blocks))[0]
    return running * (1.0 / math.sqrt(sources.shape[-1]))

def reference(surface, synthesis, analysis, stiffness, upsample, quad_weight, near_pairs, pair_count):
    highest = lax.Precision.HIGHEST
    tiles = N_TX * N_TY * N_TZ
    own_cells = surface.reshape(tiles * CPD, 3, NP)
    coeffs = jnp.einsum('qp,ckp->ckq', analysis, own_cells, precision=highest) * stiffness
    bend_force = jnp.einsum('pq,ckq->ckp', synthesis, coeffs, precision=highest)
    source_pos = jnp.einsum('up,ckp->cku', upsample, own_cells, precision=highest)
    source_den = jnp.einsum('up,ckp->cku', upsample, bend_force, precision=highest)
    slot_table = near_pairs.reshape(tiles, PD, 3)
    tile_id = jnp.broadcast_to(jnp.arange(tiles, dtype=jnp.int32)[:, None], (tiles, PD))
    slot_id = jnp.broadcast_to(jnp.arange(PD, dtype=jnp.int32)[None, :], (tiles, PD))
    tile_x = tile_id // (N_TY * N_TZ)
    tile_y = tile_id // N_TZ % N_TY
    tile_z = tile_id % N_TZ
    near_code = slot_table[:, :, 1]
    shift_x = near_code // 9 - 1
    shift_y = near_code // 3 % 3 - 1
    shift_z = near_code % 3 - 1
    other_tile = ((tile_x + shift_x) * N_TY + (tile_y + shift_y)) * N_TZ + (tile_z + shift_z)
    first_ids = (tile_id * CPD + slot_table[:, :, 0]).reshape(-1).astype(jnp.int32)
    second_ids = (other_tile * CPD + slot_table[:, :, 2]).reshape(-1).astype(jnp.int32)
    counts = pair_count.reshape(tiles)
    slot_used = (slot_id < counts[:, None]).astype(jnp.float32).reshape(-1)

    def per_pair(pair_item):
        first, second, weight = pair_item
        on_first = stokes_velocity(own_cells[first], source_pos[second], source_den[second], quad_weight) * weight
        on_second = stokes_velocity(own_cells[second], source_pos[first], source_den[first], quad_weight) * weight
        return (on_first, on_second)
    on_first, on_second = lax.map(per_pair, (first_ids, second_ids, slot_used))
    velocity = 0.25 * bend_force
    velocity = velocity.at[first_ids].add(on_first)
    velocity = velocity.at[second_ids].add(on_second)
    return velocity.reshape(surface.shape)
```

```python
import functools
import math

import jax
import jax.numpy as jnp
from jax import lax
from jax.experimental import pallas as pl
from jax.experimental.pallas import tpu as pltpu
from jax.sharding import PartitionSpec as P

MESH = pl.DeviceIdType.MESH
F32 = jnp.float32
BF16 = jnp.bfloat16
smooth_sq = 0.25

CELLS = 4
POINTS = 312
RAISED = 1248
SLOTS = 16
LANES = 128
PW = 384
RW = 1280
OWN = 13
LIST = 512
GROUP = 32
DEPTH = 80


def split2(x):
    high = x.astype(BF16)
    return high, (x - high.astype(F32)).astype(BF16)


def split3(x):
    a = x.astype(BF16).astype(F32)
    rest = x - a
    b = rest.astype(BF16).astype(F32)
    return a, b, rest - b


def dot_nt(a, b, precision=None):
    return lax.dot_general(
        a, b, (((1,), (1,)), ((), ())), preferred_element_type=F32, precision=precision
    )


def dot_nt3(a, b_high, b_low):
    high, low = split2(a)
    return dot_nt(high, b_high) + dot_nt(low, b_high) + dot_nt(high, b_low)


def exchange_kernel(
    surface, pairs, count, synthesis, analysis, stiffness, upsample,
    halo, table, target, own_bend, bend_high, bend_low, up_high, up_low,
    code_s, near_s, far_s, rows_s, own_s, send_sem, recv_sem,
):
    sizes = [lax.axis_size(a) for a in ("tx", "ty", "tz")]
    here = [lax.axis_index(a) for a in ("tx", "ty", "tz")]
    others = [n for n in range(27) if n != OWN]

    def at(n):
        step = (n // 9 - 1, n // 3 % 3 - 1, n % 3 - 1)
        return tuple(lax.rem(h + d + s, s) for h, d, s in zip(here, step, sizes))

    barrier = pltpu.get_barrier_semaphore()
    for n in others:
        pl.semaphore_signal(barrier, inc=1, device_id=at(n), device_id_type=MESH)

    own_s[...] = jnp.zeros((16, PW), F32)
    for c in range(CELLS):
        own_s[4 * c : 4 * c + 3, :POINTS] = surface[c]
    used = count[0]
    slot_row = lax.broadcasted_iota(jnp.int32, (SLOTS, LANES), 0)
    slot_lane = lax.broadcasted_iota(jnp.int32, (SLOTS, LANES), 1)
    columns = pairs[...].astype(F32)
    lane = lax.broadcasted_iota(jnp.int32, (1, LANES), 1)
    for k in range(3):
        column = jnp.broadcast_to(columns[:, k : k + 1], (SLOTS, LANES))
        row = jnp.sum(jnp.where(slot_row == slot_lane, column, 0.0), axis=0, keepdims=True)
        if k == 1:
            row = jnp.where(lane < used, row, -1.0)
        own_s[4 * k + 3 : 4 * k + 4, :LANES] = row
    for c in range(CELLS):
        halo[OWN, c] = own_s[4 * c : 4 * c + 4, :]

    pl.semaphore_wait(barrier, 26)

    copies = []
    for n in others:
        copy = pltpu.make_async_remote_copy(
            src_ref=halo.at[OWN],
            dst_ref=halo.at[26 - n],
            send_sem=send_sem.at[n],
            recv_sem=recv_sem.at[26 - n],
            device_id=at(n),
            device_id_type=MESH,
        )
        copy.start()
        copies.append(copy)

    highest = lax.Precision.HIGHEST
    bend = jnp.dot(
        synthesis[...] * stiffness[...], analysis[...],
        preferred_element_type=F32, precision=highest,
    )
    bend_high[...], bend_low[...] = split2(bend)
    own = own_s[...]
    own_bend[...] = dot_nt(own[:, :POINTS], bend, highest)
    raised = upsample[...]
    up_high[:RAISED, :], up_low[:RAISED, :] = split2(raised)
    up_high[RAISED:, :] = jnp.zeros((RW - RAISED, POINTS), BF16)
    up_low[RAISED:, :] = jnp.zeros((RW - RAISED, POINTS), BF16)
    ones = jnp.ones((3, PW), F32)
    for c in range(CELLS):
        t = own[4 * c : 4 * c + 3, :]
        norm = jnp.sum(t * t, axis=0, keepdims=True) + smooth_sq
        t1, t2, t3 = split3(t)
        s1, s2, s3 = split3(norm)
        for kind in range(2):
            at_row = 4 * kind
            scale = 1.0 if kind else -2.0
            rows_s[...] = jnp.zeros((LANES, PW), F32)
            for block, part in enumerate((t1, t1, t2, t2, t1, t3)):
                rows_s[8 * block + at_row : 8 * block + at_row + 3, :] = part * scale
            for block in (6, 7, 8):
                rows_s[8 * block + at_row : 8 * block + at_row + 3, :] = -ones if kind else ones
            if not kind:
                rows_s[72:73, :] = s1
                rows_s[73:74, :] = s2
                rows_s[74:75, :] = s3
            target[c, kind] = jnp.transpose(rows_s[...])[:POINTS].astype(BF16)

    for copy in copies:
        copy.wait_recv()

    for ref, k in ((near_s, 0), (code_s, 1), (far_s, 2)):
        ref[...] = jnp.full((LANES, LANES), -1.0, F32)
        for n in range(27):
            ref[n : n + 1, :] = halo[n, k, 3:4, :LANES]
        ref[27:28, :] = halo[OWN, k, 3:4, :LANES]
    place = lax.broadcasted_iota(jnp.int32, (32, LANES), 0)
    place_f = place.astype(F32)
    lane32 = lax.broadcasted_iota(jnp.int32, (32, LANES), 1)
    code, near, far = code_s[:32, :], near_s[:32, :], far_s[:32, :]
    mask = jnp.logical_or(
        jnp.logical_and(place < 27, code == 26.0 - place_f),
        jnp.logical_and(place == 27, code >= 0.0),
    )
    mask = jnp.logical_and(mask, lane32 < SLOTS)
    value = jnp.where(
        place == 27, near * 128.0 + (code * 4.0 + far), far * 128.0 + (place_f * 4.0 + near)
    )
    taken = mask.astype(F32)
    upper = (
        lax.broadcasted_iota(jnp.int32, (LANES, LANES), 0)
        < lax.broadcasted_iota(jnp.int32, (LANES, LANES), 1)
    ).astype(F32)
    lower = (
        lax.broadcasted_iota(jnp.int32, (32, 32), 1) < lax.broadcasted_iota(jnp.int32, (32, 32), 0)
    ).astype(F32)
    per_row = jnp.broadcast_to(jnp.sum(taken, axis=1, keepdims=True), (32, LANES))
    before = jnp.dot(taken, upper, preferred_element_type=F32)
    above = jnp.dot(lower, per_row, preferred_element_type=F32)
    code_s[:32, :] = jnp.where(mask, before + above, -1.0)
    near_s[:32, :] = value
    spot = jnp.transpose(code_s[...])[:SLOTS]
    value = jnp.transpose(near_s[...])[:SLOTS]
    index = lax.broadcasted_iota(jnp.int32, (SLOTS, LIST), 1).astype(F32)
    listed = jnp.zeros((SLOTS, LIST), F32)
    for n in range(28):
        listed = listed + jnp.where(spot[:, n : n + 1] == index, value[:, n : n + 1], 0.0)
    table[0:1, :] = jnp.sum(listed, axis=0, keepdims=True).astype(jnp.int32)
    total = jnp.sum(jnp.sum(taken, axis=1, keepdims=True), axis=0, keepdims=True)
    table[1:2, :] = jnp.broadcast_to(total, (1, LIST)).astype(jnp.int32)

    for copy in copies:
        copy.wait_send()


def sums_kernel(
    table, halo, target, own_bend, bend_high, bend_low, up_high, up_low, weight,
    velocity,
    source_s, raised_s, wide_s, square_s, along_s, total_s,
):
    count = table[1, 0]
    total_s[...] = jnp.zeros(total_s.shape, F32)
    row8 = lax.broadcasted_iota(jnp.int32, (8, RW), 0)

    def group(g, carry):
        first = g * GROUP
        last = jnp.minimum(first + GROUP, count)

        def pick(e, carry):
            cell = table[0, jnp.minimum(first + e, count - 1)] % 128
            rows = halo[cell // 4, cell % 4]
            source_s[e, 0:4, :] = rows
            source_s[e, 4:8, :] = rows
            return carry

        lax.fori_loop(0, GROUP, pick, 0)
        picked = source_s[...].reshape(GROUP * 8, PW)[:, :POINTS]
        bent = dot_nt3(picked, bend_high[...], bend_low[...])
        is_pos = lax.broadcasted_iota(jnp.int32, (GROUP * 8, POINTS), 0) % 8 < 4
        carried = jnp.where(is_pos, picked, bent)
        raised = dot_nt3(carried, up_high[...], up_low[...])
        raised_s[...] = raised.reshape(GROUP, 8, RW)

        def one(e, carry):
            item = table[0, first + e]
            cell = item // 128
            scale = jnp.where(row8 < 4, 1.0, weight[...])
            both = raised_s[e] * scale
            for c in range(3):
                wide_s[c] = jnp.broadcast_to(both[c : c + 1, :], (8, RW))
                wide_s[3 + c] = jnp.broadcast_to(both[4 + c : 5 + c, :], (8, RW))
            p1, p2, p3 = split3(both)
            m1, m2, m3 = split3(both * jnp.where(row8 < 4, both, pltpu.roll(both, 4, 0)))
            operand = jnp.concatenate(
                [p1, p2, p1, p2, p3, p1, m1, m2, m3, jnp.ones((8, RW), F32)], axis=0
            ).astype(BF16)
            square_s[...] = jnp.dot(target[cell, 0, :, :DEPTH], operand, preferred_element_type=F32)
            along_s[...] = jnp.dot(target[cell, 1, :, :DEPTH], operand, preferred_element_type=F32)

            def block(i, carry):
                at = pl.ds(pl.multiple_of(i * 8, 8), 8)
                inverse = lax.rsqrt(square_s[at, :])
                factor = along_s[at, :] * inverse * (inverse * inverse)

                def fold(x):
                    out = x[:, :LANES]
                    for k in range(1, RW // LANES):
                        out = out + x[:, k * LANES : (k + 1) * LANES]
                    return out

                total_s[cell, 3, at, :] += fold(factor)
                for c in range(3):
                    total_s[cell, c, at, :] += fold(wide_s[3 + c] * inverse - wide_s[c] * factor)
                return carry

            lax.fori_loop(0, POINTS // 8, block, 0)
            return carry

        lax.fori_loop(0, last - first, one, 0)
        return carry

    lax.fori_loop(0, (count + GROUP - 1) // GROUP, group, 0)

    ones = jnp.ones((8, LANES), BF16)

    def reduced(x):
        high, low = split2(x)
        return (dot_nt(ones, high) + dot_nt(ones, low))[0:1, :]

    for c in range(CELLS):
        weight_sum = reduced(total_s[c, 3])
        for k in range(3):
            row = 4 * c + k
            place = halo[OWN, c, k : k + 1, :POINTS]
            velocity[c, k : k + 1, :] = (
                0.25 * own_bend[row : row + 1, :]
                + reduced(total_s[c, k])
                + place * weight_sum
            )


VMEM = pl.BlockSpec(memory_space=pltpu.VMEM)
SMEM = pl.BlockSpec(memory_space=pltpu.SMEM)


def sums(table, halo, target, own_bend, bend_high, bend_low, up_high, up_low, weight):
    return pl.pallas_call(
        sums_kernel,
        out_shape=jax.ShapeDtypeStruct((CELLS, 3, POINTS), F32),
        in_specs=[SMEM] + [VMEM] * 8,
        out_specs=VMEM,
        scratch_shapes=[
            pltpu.VMEM((GROUP, 8, PW), F32),
            pltpu.VMEM((GROUP, 8, RW), F32),
            pltpu.VMEM((6, 8, RW), F32),
            pltpu.VMEM((POINTS, RW), F32),
            pltpu.VMEM((POINTS, RW), F32),
            pltpu.VMEM((CELLS, 4, POINTS, LANES), F32),
        ],
        compiler_params=pltpu.CompilerParams(vmem_limit_bytes=40 * 2**20),
        name="sums",
    )(table, halo, target, own_bend, bend_high, bend_low, up_high, up_low, weight)


def shards(surface, synthesis, analysis, stiffness, upsample, quad_weight, near_pairs, pair_count):
    outs = pl.pallas_call(
        exchange_kernel,
        out_shape=(
            jax.ShapeDtypeStruct((27, CELLS, 4, PW), F32),
            jax.ShapeDtypeStruct((2, LIST), jnp.int32),
            jax.ShapeDtypeStruct((CELLS, 2, POINTS, LANES), BF16),
            jax.ShapeDtypeStruct((16, POINTS), F32),
            jax.ShapeDtypeStruct((POINTS, POINTS), BF16),
            jax.ShapeDtypeStruct((POINTS, POINTS), BF16),
            jax.ShapeDtypeStruct((RW, POINTS), BF16),
            jax.ShapeDtypeStruct((RW, POINTS), BF16),
        ),
        in_specs=[VMEM, VMEM, SMEM] + [VMEM] * 4,
        out_specs=[VMEM] * 8,
        scratch_shapes=[
            pltpu.VMEM((LANES, LANES), F32),
            pltpu.VMEM((LANES, LANES), F32),
            pltpu.VMEM((LANES, LANES), F32),
            pltpu.VMEM((LANES, PW), F32),
            pltpu.VMEM((16, PW), F32),
            pltpu.SemaphoreType.DMA((27,)),
            pltpu.SemaphoreType.DMA((27,)),
        ],
        compiler_params=pltpu.CompilerParams(
            collective_id=0, has_side_effects=True, vmem_limit_bytes=40 * 2**20
        ),
        name="exchange",
    )(
        surface[0, 0, 0], near_pairs[0, 0, 0], pair_count.reshape(1),
        synthesis, analysis, stiffness[None, :], upsample,
    )
    halo, table, *prepared = outs
    weight = jnp.pad(quad_weight * (1.0 / math.sqrt(RAISED)), (0, RW - RAISED))[None, :]
    velocity = sums(table, halo, *prepared, weight)
    return velocity[None, None, None]


def solution(mesh):
    return jax.shard_map(
        shards,
        mesh=mesh,
        in_specs=(
            P("tx", "ty", "tz", None, None, None),
            P(),
            P(),
            P(),
            P(),
            P(),
            P("tx", "ty", "tz", None, None),
            P("tx", "ty", "tz"),
        ),
        out_specs=P("tx", "ty", "tz", None, None, None),
        check_vma=False,
    )
```

```python
import functools
import math

import jax
import jax.numpy as jnp
from jax import lax
from jax.experimental import pallas as pl
from jax.experimental.pallas import tpu as pltpu
from jax.sharding import PartitionSpec as P

MESH = pl.DeviceIdType.MESH
F32 = jnp.float32
BF16 = jnp.bfloat16
smooth_sq = 0.25

CELLS = 4
POINTS = 312
RAISED = 1248
SLOTS = 16
LANES = 128
PW = 384
RW = 1280
OWN = 13
LIST = 512
GROUP = 32
DEPTH = 80


def split2(x):
    high = x.astype(BF16)
    return high, (x - high.astype(F32)).astype(BF16)


def split3(x):
    a = x.astype(BF16).astype(F32)
    rest = x - a
    b = rest.astype(BF16).astype(F32)
    return a, b, rest - b


def dot_nt(a, b):
    return lax.dot_general(a, b, (((1,), (1,)), ((), ())), preferred_element_type=F32)


def dot(a, b, precision=None):
    return jnp.dot(a, b, preferred_element_type=F32, precision=precision)


def dot3(a, b_high, b_low):
    high, low = split2(a)
    return dot(high, b_high) + dot(low, b_high) + dot(high, b_low)


def exchange_kernel(
    surface, pairs, count, synthesis, analysis, stiffness, upsample,
    halo, table, target, own_place, own_bend, bend_high, bend_low, up_high, up_low,
    code_s, near_s, far_s, rows_s, own_s, slots_s, raise_s, raise_sem, send_sem, recv_sem,
):
    sizes = [lax.axis_size(a) for a in ("tx", "ty", "tz")]
    here = [lax.axis_index(a) for a in ("tx", "ty", "tz")]
    others = [n for n in range(27) if n != OWN]

    def at(n):
        step = (n // 9 - 1, n // 3 % 3 - 1, n % 3 - 1)
        return tuple(lax.rem(h + d + s, s) for h, d, s in zip(here, step, sizes))

    fetch = pltpu.make_async_copy(upsample, raise_s, raise_sem)
    fetch.start()
    barrier = pltpu.get_barrier_semaphore()
    for n in others:
        pl.semaphore_signal(barrier, inc=1, device_id=at(n), device_id_type=MESH)

    own_s[...] = jnp.zeros((16, PW), F32)
    for c in range(CELLS):
        for k in range(3):
            own_s[4 * c + k : 4 * c + k + 1, :POINTS] = surface[k, c : c + 1, :]
    used = count[0]
    lane = lax.broadcasted_iota(jnp.int32, (1, LANES), 1)
    for c in range(CELLS):
        at_row = 4 * c
        halo[OWN, c, 0:3] = own_s[at_row : at_row + 3, :LANES]
        halo[OWN, c, 3:6] = own_s[at_row : at_row + 3, LANES : 2 * LANES]
        halo[OWN, c, 6:7] = own_s[at_row : at_row + 1, 2 * LANES :] + pltpu.roll(
            own_s[at_row + 1 : at_row + 2, 2 * LANES :], 64, 1
        )
        row = own_s[at_row + 2 : at_row + 3, 2 * LANES :]
        if c < 3:
            slots_s[...] = jnp.full((1, LANES), -1.0, F32)
            slots_s[:, :SLOTS] = pairs[c].astype(F32)
            pair = slots_s[...]
            if c == 1:
                pair = jnp.where(lane < used, pair, -1.0)
            pair = pltpu.roll(jnp.where(lane < SLOTS, pair, 0.0), 64, 1)
            row = row + pair
        halo[OWN, c, 7:8] = row

    pl.semaphore_wait(barrier, 26)

    copies = []
    for n in others:
        copy = pltpu.make_async_remote_copy(
            src_ref=halo.at[OWN],
            dst_ref=halo.at[26 - n],
            send_sem=send_sem.at[n],
            recv_sem=recv_sem.at[26 - n],
            device_id=at(n),
            device_id_type=MESH,
        )
        copy.start()
        copies.append(copy)

    highest = lax.Precision.HIGHEST
    modes = analysis.shape[0]
    diagonal = lax.broadcasted_iota(jnp.int32, (modes, modes), 0) == lax.broadcasted_iota(
        jnp.int32, (modes, modes), 1
    )
    stiff = jnp.sum(jnp.where(diagonal, stiffness[...], 0.0), axis=1, keepdims=True)
    bend = lax.dot_general(
        analysis[...] * stiff, synthesis[...], (((0,), (0,)), ((), ())),
        preferred_element_type=F32, precision=highest,
    )
    bend_high[...], bend_low[...] = split2(bend)
    own = own_s[...]
    own_bend[...] = dot(own[:, :POINTS], bend, highest)
    fetch.wait()
    up_high[:, :RAISED], up_low[:, :RAISED] = split2(raise_s[...])
    up_high[:, RAISED:] = jnp.zeros((POINTS, RW - RAISED), BF16)
    up_low[:, RAISED:] = jnp.zeros((POINTS, RW - RAISED), BF16)
    own_place[...] = own[:, :POINTS]
    ones = jnp.ones((3, PW), F32)
    for c in range(CELLS):
        t = own[4 * c : 4 * c + 3, :]
        norm = jnp.sum(t * t, axis=0, keepdims=True) + smooth_sq
        t1, t2, t3 = split3(t)
        s1, s2, s3 = split3(norm)
        for kind in range(2):
            at_row = 4 * kind
            scale = 1.0 if kind else -2.0
            rows_s[...] = jnp.zeros((LANES, PW), F32)
            for block, part in enumerate((t1, t1, t2, t2, t1, t3)):
                rows_s[8 * block + at_row : 8 * block + at_row + 3, :] = part * scale
            for block in (6, 7, 8):
                rows_s[8 * block + at_row : 8 * block + at_row + 3, :] = -ones if kind else ones
            if not kind:
                rows_s[72:73, :] = s1
                rows_s[73:74, :] = s2
                rows_s[74:75, :] = s3
            target[c, kind] = jnp.transpose(rows_s[...])[:POINTS].astype(BF16)

    for copy in copies:
        copy.wait_recv()

    for ref, k in ((near_s, 0), (code_s, 1), (far_s, 2)):
        ref[...] = jnp.full((LANES, LANES), -1.0, F32)
        for n in range(27):
            ref[n : n + 1, :] = halo[n, k, 7:8, :]
        ref[27:28, :] = halo[OWN, k, 7:8, :]
    place = lax.broadcasted_iota(jnp.int32, (32, LANES), 0)
    place_f = place.astype(F32)
    lane32 = lax.broadcasted_iota(jnp.int32, (32, LANES), 1)
    code, near, far = code_s[:32, :], near_s[:32, :], far_s[:32, :]
    mask = jnp.logical_or(
        jnp.logical_and(place < 27, code == 26.0 - place_f),
        jnp.logical_and(place == 27, code >= 0.0),
    )
    mask = jnp.logical_and(mask, jnp.logical_and(lane32 >= 64, lane32 < 64 + SLOTS))
    value = jnp.where(
        place == 27, near * 128.0 + (code * 4.0 + far), far * 128.0 + (place_f * 4.0 + near)
    )
    taken = mask.astype(F32)
    upper = (
        lax.broadcasted_iota(jnp.int32, (LANES, LANES), 0)
        < lax.broadcasted_iota(jnp.int32, (LANES, LANES), 1)
    ).astype(F32)
    lower = (
        lax.broadcasted_iota(jnp.int32, (32, 32), 1) < lax.broadcasted_iota(jnp.int32, (32, 32), 0)
    ).astype(F32)
    per_row = jnp.broadcast_to(jnp.sum(taken, axis=1, keepdims=True), (32, LANES))
    before = jnp.dot(taken, upper, preferred_element_type=F32)
    above = jnp.dot(lower, per_row, preferred_element_type=F32)
    code_s[:32, :] = jnp.where(mask, before + above, -1.0)
    near_s[:32, :] = value
    spot = jnp.transpose(code_s[...])[64 : 64 + SLOTS]
    value = jnp.transpose(near_s[...])[64 : 64 + SLOTS]
    index = lax.broadcasted_iota(jnp.int32, (SLOTS, LIST), 1).astype(F32)
    listed = jnp.zeros((SLOTS, LIST), F32)
    for n in range(28):
        listed = listed + jnp.where(spot[:, n : n + 1] == index, value[:, n : n + 1], 0.0)
    table[0:1, :] = jnp.sum(listed, axis=0, keepdims=True).astype(jnp.int32)
    total = jnp.sum(jnp.sum(taken, axis=1, keepdims=True), axis=0, keepdims=True)
    table[1:2, :] = jnp.broadcast_to(total, (1, LIST)).astype(jnp.int32)

    for copy in copies:
        copy.wait_send()


def sums_kernel(
    table, halo, target, own_place, own_bend, bend_high, bend_low, up_high, up_low, weight,
    velocity,
    source_s, raised_s, wide0, wide1, forms0, forms1, total_s, operand_s,
):
    count = table[1, 0]
    wide_s, forms_s = (wide0, wide1), (forms0, forms1)
    total_s[...] = jnp.zeros(total_s.shape, F32)
    source_s[...] = jnp.zeros(source_s.shape, F32)
    row8 = lax.broadcasted_iota(jnp.int32, (8, RW), 0)

    def group(g, carry):
        first = g * GROUP
        last = jnp.minimum(first + GROUP, count)

        def pick(e, carry):
            cell = table[0, jnp.minimum(first + e, count - 1)] % 128
            tile = halo[cell // 4, cell % 4]
            for at_row in (0, 4):
                source_s[e, at_row : at_row + 3, :LANES] = tile[0:3]
                source_s[e, at_row : at_row + 3, LANES : 2 * LANES] = tile[3:6]
                source_s[e, at_row : at_row + 1, 2 * LANES :] = tile[6:7]
                source_s[e, at_row + 1 : at_row + 2, 2 * LANES :] = pltpu.roll(tile[6:7], 64, 1)
                source_s[e, at_row + 2 : at_row + 3, 2 * LANES :] = tile[7:8]
            return carry

        lax.fori_loop(0, GROUP, pick, 0)
        picked = source_s[...].reshape(GROUP * 8, PW)[:, :POINTS]
        bent = dot3(picked, bend_high[...], bend_low[...])
        is_pos = lax.broadcasted_iota(jnp.int32, (GROUP * 8, POINTS), 0) % 8 < 4
        carried = jnp.where(is_pos, picked, bent)
        raised = dot3(carried, up_high[...], up_low[...])
        raised_s[...] = raised.reshape(GROUP, 8, RW)

        def prepare(e, slot):
            both = raised_s[jnp.minimum(e, GROUP - 1)] * scale
            for c in range(3):
                wide_s[slot][c] = jnp.broadcast_to(both[c : c + 1, :], (8, RW))
                wide_s[slot][3 + c] = jnp.broadcast_to(both[4 + c : 5 + c, :], (8, RW))
            p1, p2, p3 = split3(both)
            m1, m2, m3 = split3(both * jnp.where(row8 < 4, both, pltpu.roll(both, 4, 0)))
            return jnp.concatenate(
                [p1, p2, p1, p2, p3, p1, m1, m2, m3, jnp.ones((8, RW), F32)], axis=0
            ).astype(BF16)

        def cell_of(e):
            return table[0, jnp.minimum(first + e, LIST - 1)] // 128

        def expand(e, slot, operand, step):
            lanes = slice(step * 256, step * 256 + 256)
            out = jnp.dot(
                target[cell_of(e)].reshape(2 * POINTS, LANES)[:, :DEPTH], operand[:, lanes],
                preferred_element_type=F32,
            )
            forms_s[slot][:, lanes] = out

        def fold2(cell, slot, base, begin, size):
            acc = [None] * size
            for k in range(RW // LANES):
                ln = slice(k * LANES, (k + 1) * LANES)
                ys = [wide_s[slot][c, :, ln] for c in range(3)]
                gs = [wide_s[slot][3 + c, :, ln] for c in range(3)]
                for r in range(size):
                    row = base + 8 * (begin + r)
                    inverse = lax.rsqrt(forms_s[slot][pl.ds(row, 8), ln])
                    factor = forms_s[slot][pl.ds(POINTS + row, 8), ln] * inverse * (inverse * inverse)
                    new = [gs[c] * inverse - ys[c] * factor for c in range(3)] + [factor]
                    acc[r] = new if k == 0 else [a + b for a, b in zip(acc[r], new)]
            for r in range(size):
                row = base + 8 * (begin + r)
                for c in range(4):
                    total_s[cell, c, pl.ds(row, 8), :] += acc[r][c]

        def both_slots(i, carry):
            for half in range(2):
                e = 2 * i + half
                cell = jnp.where(e < last - first, cell_of(e), CELLS)
                operand = prepare(e + 1, 1 - half)
                def chunk(q, carry):
                    base = pl.multiple_of(q * 104, 8)
                    for kind in range(2):
                        out = jnp.dot(target[cell_of(e + 1), kind, pl.ds(base, 104), :][:, :DEPTH], operand_s[...], preferred_element_type=F32)
                        forms_s[1 - half][pl.ds(kind * POINTS + base, 104), :] = out
                    for begin in range(0, 13, 3):
                        fold2(cell, half, base, begin, min(3, 13 - begin))
                    return carry
                operand_s[...] = operand
                lax.fori_loop(0, 3, chunk, 0)
            return carry

        scale = jnp.where(row8 < 4, 1.0, weight[...])
        operand = prepare(0, 0)
        for step in range(5):
            expand(0, 0, operand, step)
        lax.fori_loop(0, (last - first + 1) // 2, both_slots, 0)
        return carry

    lax.fori_loop(0, (count + GROUP - 1) // GROUP, group, 0)

    ones = jnp.ones((8, LANES), BF16)

    def reduced(x):
        high, low = split2(x)
        return (dot_nt(ones, high) + dot_nt(ones, low))[0:1, :]

    for c in range(CELLS):
        weight_sum = reduced(total_s[c, 3])
        for k in range(3):
            row = 4 * c + k
            place = own_place[row : row + 1, :]
            velocity[k, c : c + 1, :] = (
                0.25 * own_bend[row : row + 1, :]
                + reduced(total_s[c, k])
                + place * weight_sum
            )


VMEM = pl.BlockSpec(memory_space=pltpu.VMEM)
SMEM = pl.BlockSpec(memory_space=pltpu.SMEM)


def sums(table, halo, target, own_place, own_bend, bend_high, bend_low, up_high, up_low, weight):
    return pl.pallas_call(
        sums_kernel,
        out_shape=jax.ShapeDtypeStruct((3, CELLS, POINTS), F32),
        in_specs=[SMEM] + [VMEM] * 9,
        out_specs=VMEM,
        scratch_shapes=[
            pltpu.VMEM((GROUP, 8, PW), F32),
            pltpu.VMEM((GROUP, 8, RW), F32),
            pltpu.VMEM((6, 8, RW), F32),
            pltpu.VMEM((6, 8, RW), F32),
            pltpu.VMEM((2 * POINTS, RW), F32),
            pltpu.VMEM((2 * POINTS, RW), F32),
            pltpu.VMEM((CELLS + 1, 4, POINTS, LANES), F32),
            pltpu.VMEM((DEPTH, RW), BF16),
        ],
        compiler_params=pltpu.CompilerParams(vmem_limit_bytes=40 * 2**20),
        name="sums",
    )(table, halo, target, own_place, own_bend, bend_high, bend_low, up_high, up_low, weight)


def shards(surface, synthesis, analysis, stiffness, upsample, quad_weight, near_pairs, pair_count):
    outs = pl.pallas_call(
        exchange_kernel,
        out_shape=(
            jax.ShapeDtypeStruct((27, CELLS, 8, LANES), F32),
            jax.ShapeDtypeStruct((2, LIST), jnp.int32),
            jax.ShapeDtypeStruct((CELLS, 2, POINTS, LANES), BF16),
            jax.ShapeDtypeStruct((16, POINTS), F32),
            jax.ShapeDtypeStruct((16, POINTS), F32),
            jax.ShapeDtypeStruct((POINTS, POINTS), BF16),
            jax.ShapeDtypeStruct((POINTS, POINTS), BF16),
            jax.ShapeDtypeStruct((POINTS, RW), BF16),
            jax.ShapeDtypeStruct((POINTS, RW), BF16),
        ),
        in_specs=[VMEM, VMEM, SMEM] + [VMEM] * 3 + [pl.BlockSpec(memory_space=pltpu.HBM)],
        out_specs=[VMEM] * 9,
        scratch_shapes=[
            pltpu.VMEM((LANES, LANES), F32),
            pltpu.VMEM((LANES, LANES), F32),
            pltpu.VMEM((LANES, LANES), F32),
            pltpu.VMEM((LANES, PW), F32),
            pltpu.VMEM((16, PW), F32),
            pltpu.VMEM((1, LANES), F32),
            pltpu.VMEM((POINTS, RAISED), F32),
            pltpu.SemaphoreType.DMA,
            pltpu.SemaphoreType.DMA((27,)),
            pltpu.SemaphoreType.DMA((27,)),
        ],
        compiler_params=pltpu.CompilerParams(
            collective_id=0, has_side_effects=True, vmem_limit_bytes=40 * 2**20
        ),
        name="exchange",
    )(
        jnp.swapaxes(surface[0, 0, 0], 0, 1), near_pairs[0, 0, 0].T[:, None, :], pair_count.reshape(1),
        synthesis.T, analysis, stiffness[None, :], upsample.T,
    )
    halo, table, *prepared = outs
    weight = jnp.pad(quad_weight * (1.0 / math.sqrt(RAISED)), (0, RW - RAISED))[None, :]
    velocity = sums(table, halo, *prepared, weight)
    return jnp.swapaxes(velocity, 0, 1)[None, None, None]


def solution(mesh):
    return jax.shard_map(
        shards,
        mesh=mesh,
        in_specs=(
            P("tx", "ty", "tz", None, None, None),
            P(),
            P(),
            P(),
            P(),
            P(),
            P("tx", "ty", "tz", None, None),
            P("tx", "ty", "tz"),
        ),
        out_specs=P("tx", "ty", "tz", None, None, None),
        check_vma=False,
    )
```

```python
import functools
import math

import jax
import jax.numpy as jnp
from jax import lax
from jax.experimental import pallas as pl
from jax.experimental.pallas import tpu as pltpu
from jax.sharding import PartitionSpec as P

MESH = pl.DeviceIdType.MESH
F32 = jnp.float32
BF16 = jnp.bfloat16
smooth_sq = 0.25

CELLS = 4
POINTS = 312
RAISED = 1248
MODES = 169
SLOTS = 16
LANES = 128
PW = 384
RW = 1280
VMEM_BYTES = 63 * 2**20
OWN = 13
LIST = 512
CHUNKS = 3
CHUNK = POINTS // CHUNKS
GROUP = 32
DEPTH = 80


def split2(x):
    high = x.astype(BF16)
    return high, (x - high.astype(F32)).astype(BF16)


def split3(x):
    a = x.astype(BF16).astype(F32)
    rest = x - a
    b = rest.astype(BF16).astype(F32)
    return a, b, rest - b


def dot_nt(a, b):
    return lax.dot_general(a, b, (((1,), (1,)), ((), ())), preferred_element_type=F32)


def dot(a, b, precision=None):
    return jnp.dot(a, b, preferred_element_type=F32, precision=precision)


def split_rows(x):
    high, low = split2(x[:, :256])
    lane = lax.broadcasted_iota(jnp.int32, (x.shape[0], LANES), 1)
    rest = jnp.where(lane < 64, x[:, 256:], 0.0)
    rest_high = rest.astype(BF16).astype(F32)
    both = rest_high + pltpu.roll(rest - rest_high, 64, 1)
    return jnp.concatenate([high, low, high, both.astype(BF16), rest_high.astype(BF16)], axis=1)


def split_columns(place, x):
    width = x.shape[1]
    place[...] = jnp.zeros(place.shape, BF16)
    place[0:256, :width], place[256:512, :width] = split2(x[:256])
    rest = jnp.concatenate([x[256:], jnp.zeros((64 - (POINTS - 256), width), F32)], axis=0)
    high, low = split2(rest)
    place[512:576, :width] = high
    place[576:640, :width] = high
    place[640:704, :width] = low


def split_dot(x, place):
    whole = jnp.concatenate([place[0:256], place[0:256], place[256:512], place[512:768]], axis=0)
    return dot(x, whole)


def exchange_kernel(
    count_h, surface_h, pairs_h, synthesis_h, analysis_h, stiffness_h, upsample_h, weight_h,
    halo_h, table_h, target_h, own_h, bend_h, up_h, weight_out_h,
    halo, table, target, own_v, bend_v, up_v, weight,
    code_s, near_s, far_s, rows_s, own_s, slots_s,
    surface, pairs, synthesis, analysis, stiffness, upsample, weight_s, count,
    fetch_sem, store_sem, send_sem, recv_sem,
):
    sizes = [lax.axis_size(a) for a in ("tx", "ty", "tz")]
    here = [lax.axis_index(a) for a in ("tx", "ty", "tz")]
    others = [n for n in range(27) if n != OWN]

    def at(n):
        step = (n // 9 - 1, n // 3 % 3 - 1, n % 3 - 1)
        return tuple(lax.rem(h + d + s, s) for h, d, s in zip(here, step, sizes))

    fetches = []
    for i, (source, place) in enumerate((
        (surface_h, surface), (pairs_h, pairs), (count_h, count), (synthesis_h, synthesis),
        (analysis_h, analysis), (stiffness_h, stiffness), (upsample_h, upsample),
        (weight_h, weight_s),
    )):
        fetch = pltpu.make_async_copy(source, place, fetch_sem.at[i])
        fetch.start()
        fetches.append(fetch)
    barrier = pltpu.get_barrier_semaphore()
    for n in others:
        pl.semaphore_signal(barrier, inc=1, device_id=at(n), device_id_type=MESH)

    own_s[...] = jnp.zeros((16, PW), F32)
    for fetch in fetches[:3]:
        fetch.wait()
    for c in range(CELLS):
        for k in range(3):
            own_s[4 * c + k : 4 * c + k + 1, :POINTS] = surface[k, c : c + 1, :]
    used = count[0, 0, 0]
    lane = lax.broadcasted_iota(jnp.int32, (1, LANES), 1)
    for c in range(CELLS):
        at_row = 4 * c
        halo[4 * OWN + c, 0:3] = own_s[at_row : at_row + 3, :LANES]
        halo[4 * OWN + c, 3:6] = own_s[at_row : at_row + 3, LANES : 2 * LANES]
        halo[4 * OWN + c, 6:7] = own_s[at_row : at_row + 1, 2 * LANES :] + pltpu.roll(
            own_s[at_row + 1 : at_row + 2, 2 * LANES :], 64, 1
        )
        row = own_s[at_row + 2 : at_row + 3, 2 * LANES :]
        if c < 3:
            slots_s[...] = jnp.full((1, LANES), -1.0, F32)
            slots_s[:, :SLOTS] = pairs[0, 0, c].astype(F32)
            pair = slots_s[...]
            if c == 1:
                pair = jnp.where(lane < used, pair, -1.0)
            pair = pltpu.roll(jnp.where(lane < SLOTS, pair, 0.0), 64, 1)
            row = row + pair
        halo[4 * OWN + c, 7:8] = row

    pl.semaphore_wait(barrier, 26)

    copies = []
    for n in others:
        copy = pltpu.make_async_remote_copy(
            src_ref=halo.at[pl.ds(4 * OWN, CELLS)],
            dst_ref=halo.at[pl.ds(4 * (26 - n), CELLS)],
            send_sem=send_sem.at[n],
            recv_sem=recv_sem.at[26 - n],
            device_id=at(n),
            device_id_type=MESH,
        )
        copy.start()
        copies.append(copy)

    highest = lax.Precision.HIGHEST
    for fetch in fetches[3:]:
        fetch.wait()
    modes = analysis.shape[0]
    diagonal = lax.broadcasted_iota(jnp.int32, (modes, modes), 0) == lax.broadcasted_iota(
        jnp.int32, (modes, modes), 1
    )
    stiff = jnp.sum(jnp.where(diagonal, stiffness[...], 0.0), axis=1, keepdims=True)
    bend = lax.dot_general(
        analysis[...] * stiff, synthesis[...], (((0,), (0,)), ((), ())),
        preferred_element_type=F32, precision=highest,
    )
    split_columns(bend_v, bend)
    own = own_s[...]
    own_v[1, :, :POINTS] = dot(own[:, :POINTS], bend, highest)
    split_columns(up_v, upsample[...])
    own_v[0] = own
    weight[...] = jnp.ones((8, RW), F32)
    weight[4:8, :RAISED] = jnp.broadcast_to(weight_s[...][None, :] * (1.0 / math.sqrt(RAISED)), (4, RAISED))
    ones = jnp.ones((3, PW), F32)
    for c in range(CELLS):
        t = own[4 * c : 4 * c + 3, :]
        norm = jnp.sum(t * t, axis=0, keepdims=True) + smooth_sq
        t1, t2, t3 = split3(t)
        s1, s2, s3 = split3(norm)
        forms = []
        for kind in range(2):
            at_row = 4 * kind
            scale = 1.0 if kind else -2.0
            rows_s[...] = jnp.zeros((LANES, PW), F32)
            for block, part in enumerate((t1, t1, t2, t2, t1, t3)):
                rows_s[8 * block + at_row : 8 * block + at_row + 3, :] = part * scale
            for block in (6, 7, 8):
                rows_s[8 * block + at_row : 8 * block + at_row + 3, :] = -ones if kind else ones
            if not kind:
                rows_s[72:73, :] = s1
                rows_s[73:74, :] = s2
                rows_s[74:75, :] = s3
            forms.append(jnp.transpose(rows_s[...]))
        for q in range(CHUNKS):
            rows = slice(q * CHUNK, (q + 1) * CHUNK)
            target[c, q] = jnp.concatenate([forms[0][rows], forms[1][rows]], axis=0).astype(BF16)
    stores = []

    def store(place, out):
        copy = pltpu.make_async_copy(place, out, store_sem.at[len(stores)])
        copy.start()
        stores.append(copy)

    store(target, target_h)
    store(own_v, own_h)
    store(bend_v, bend_h)
    store(up_v, up_h)
    store(weight, weight_out_h)

    for copy in copies:
        copy.wait_recv()
    store(halo, halo_h)

    for ref, k in ((near_s, 0), (code_s, 1), (far_s, 2)):
        ref[...] = jnp.full((LANES, LANES), -1.0, F32)
        for n in range(27):
            ref[n : n + 1, :] = halo[4 * n + k, 7:8, :]
        ref[27:28, :] = halo[4 * OWN + k, 7:8, :]
    place = lax.broadcasted_iota(jnp.int32, (32, LANES), 0)
    place_f = place.astype(F32)
    lane32 = lax.broadcasted_iota(jnp.int32, (32, LANES), 1)
    code, near, far = code_s[:32, :], near_s[:32, :], far_s[:32, :]
    mask = jnp.logical_or(
        jnp.logical_and(place < 27, code == 26.0 - place_f),
        jnp.logical_and(place == 27, code >= 0.0),
    )
    mask = jnp.logical_and(mask, jnp.logical_and(lane32 >= 64, lane32 < 64 + SLOTS))
    value = jnp.where(
        place == 27, near * 128.0 + (code * 4.0 + far), far * 128.0 + (place_f * 4.0 + near)
    )
    taken = mask.astype(F32)
    upper = (
        lax.broadcasted_iota(jnp.int32, (LANES, LANES), 0)
        < lax.broadcasted_iota(jnp.int32, (LANES, LANES), 1)
    ).astype(F32)
    lower = (
        lax.broadcasted_iota(jnp.int32, (32, 32), 1) < lax.broadcasted_iota(jnp.int32, (32, 32), 0)
    ).astype(F32)
    per_row = jnp.broadcast_to(jnp.sum(taken, axis=1, keepdims=True), (32, LANES))
    before = jnp.dot(taken, upper, preferred_element_type=F32)
    above = jnp.dot(lower, per_row, preferred_element_type=F32)
    code_s[:32, :] = jnp.where(mask, before + above, -1.0)
    near_s[:32, :] = value
    spot = jnp.transpose(code_s[...])[64 : 64 + SLOTS]
    value = jnp.transpose(near_s[...])[64 : 64 + SLOTS]
    index = lax.broadcasted_iota(jnp.int32, (SLOTS, LIST), 1).astype(F32)
    listed = jnp.zeros((SLOTS, LIST), F32)
    for n in range(28):
        listed = listed + jnp.where(spot[:, n : n + 1] == index, value[:, n : n + 1], 0.0)
    table[0:1, :] = jnp.sum(listed, axis=0, keepdims=True).astype(jnp.int32)
    total = jnp.sum(jnp.sum(taken, axis=1, keepdims=True), axis=0, keepdims=True)
    table[1:2, :] = jnp.broadcast_to(total, (1, LIST)).astype(jnp.int32)

    store(table, table_h)
    for copy in stores:
        copy.wait()
    for copy in copies:
        copy.wait_send()


def sums_kernel(
    table_h, halo_h, target_h, own_h, bend_h, up_h, weight_h,
    velocity,
    table, halo, target, own, bend, up, weight, fetch_sem,
    source_s, raised_s, wide0, wide1, forms0, forms1, total_s, operand_s,
):
    fetches = []
    for i, (source, place) in enumerate((
        (table_h, table), (halo_h, halo), (bend_h, bend), (up_h, up),
        (weight_h, weight), (target_h, target), (own_h, own),
    )):
        fetch = pltpu.make_async_copy(source, place, fetch_sem.at[i])
        fetch.start()
        fetches.append(fetch)
    wide_s, forms_s = (wide0, wide1), (forms0, forms1)
    total_s[...] = jnp.zeros(total_s.shape, F32)
    source_s[...] = jnp.zeros(source_s.shape, F32)
    for fetch in fetches:
        fetch.wait()
    count = table[1, 0]
    row8 = lax.broadcasted_iota(jnp.int32, (8, RW), 0)

    def group(g, carry):
        first = g * GROUP
        last = jnp.minimum(first + GROUP, count)

        for e in range(GROUP):
            tile = halo[table[0, first + e] % 128]
            at_row = e % 2 * 4
            source_s[e // 2, at_row : at_row + 3, :LANES] = tile[0:3]
            source_s[e // 2, at_row : at_row + 3, LANES : 2 * LANES] = tile[3:6]
            source_s[e // 2, at_row : at_row + 1, 2 * LANES :] = tile[6:7]
            source_s[e // 2, at_row + 1 : at_row + 2, 2 * LANES :] = pltpu.roll(tile[6:7], 64, 1)
            source_s[e // 2, at_row + 2 : at_row + 3, 2 * LANES :] = tile[7:8]
        places = split_rows(source_s[...].reshape(GROUP * 4, PW))
        bent = split_rows(split_dot(places, bend))
        raised = split_dot(jnp.concatenate([places, bent], axis=0), up)
        raised_s[...] = raised.reshape(2, GROUP // 2, 8, RW)

        def prepare(block, odd, slot):
            block = jnp.minimum(block, GROUP // 2 - 1)
            places, forces = raised_s[0, block], raised_s[1, block]
            if odd:
                places = pltpu.roll(places, 4, 0)
            else:
                forces = pltpu.roll(forces, 4, 0)
            both = jnp.where(row8 < 4, places, forces) * weight[...]
            for c in range(3):
                wide_s[slot][c] = jnp.broadcast_to(both[c : c + 1, :], (8, RW))
                wide_s[slot][3 + c] = jnp.broadcast_to(both[4 + c : 5 + c, :], (8, RW))
            p1, p2, p3 = split3(both)
            m1, m2, m3 = split3(both * jnp.where(row8 < 4, both, pltpu.roll(both, 4, 0)))
            operand_s[...] = jnp.concatenate(
                [p1, p2, p1, p2, p3, p1, m1, m2, m3, jnp.ones((8, RW), F32)], axis=0
            ).astype(BF16)

        def cell_of(e):
            return table[0, first + e] // 128

        def expand(cell, slot, q):
            forms_s[slot][q] = dot(target[cell, q][:, :DEPTH], operand_s[...])

        def fold(cell, slot, q, begin, size):
            acc = [None] * size
            for k in range(RW // LANES):
                ln = slice(k * LANES, (k + 1) * LANES)
                ys = [wide_s[slot][c, :, ln] for c in range(3)]
                gs = [wide_s[slot][3 + c, :, ln] for c in range(3)]
                for r in range(size):
                    row = 8 * (begin + r)
                    inverse = lax.rsqrt(forms_s[slot][q, row : row + 8, ln])
                    along = forms_s[slot][q, CHUNK + row : CHUNK + row + 8, ln]
                    factor = along * inverse * (inverse * inverse)
                    new = [gs[c] * inverse - ys[c] * factor for c in range(3)] + [factor]
                    acc[r] = new if k == 0 else [a + b for a, b in zip(acc[r], new)]
            for r in range(size):
                row = 8 * (begin + r)
                for c in range(4):
                    total_s[cell, c, q, row : row + 8, :] += acc[r][c]

        def two(i, carry):
            for half in range(2):
                e = 2 * i + half
                cell = jnp.where(e < last - first, cell_of(e), CELLS)
                later = cell_of(e + 1)
                prepare(i + half, 1 - half, 1 - half)

                def chunk(q, carry):
                    expand(later, 1 - half, q)
                    for begin in range(0, CHUNK // 8, 3):
                        fold(cell, half, q, begin, min(3, CHUNK // 8 - begin))
                    return carry

                lax.fori_loop(0, CHUNKS, chunk, 0)
            return carry

        prepare(0, 0, 0)
        for q in range(CHUNKS):
            expand(cell_of(0), 0, q)
        lax.fori_loop(0, (last - first + 1) // 2, two, 0)
        return carry

    lax.fori_loop(0, (count + GROUP - 1) // GROUP, group, 0)

    ones = jnp.ones((8, LANES), BF16)

    def reduced(x):
        high, low = split2(x)
        return (dot_nt(ones, high) + dot_nt(ones, low))[0:1, :]

    for c in range(CELLS):
        weight_sum = reduced(total_s[c, 3].reshape(POINTS, LANES))
        for k in range(3):
            row = 4 * c + k
            place = own[0, row : row + 1, :POINTS]
            velocity[k, c : c + 1, :] = (
                0.25 * own[1, row : row + 1, :POINTS]
                + reduced(total_s[c, k].reshape(POINTS, LANES))
                + place * weight_sum
            )


HBM = pl.BlockSpec(memory_space=pltpu.HBM)

HANDED = (
    ((27 * CELLS, 8, LANES), F32),
    ((2, LIST), jnp.int32),
    ((CELLS, CHUNKS, 2 * CHUNK, LANES), BF16),
    ((2, 16, PW), F32),
    ((768, PW), BF16),
    ((768, RW), BF16),
    ((8, RW), F32),
)


def sums(halo, table, target, own, bend, up, weight):
    held = [pltpu.VMEM(*h) for h in HANDED]
    return pl.pallas_call(
        sums_kernel,
        out_shape=jax.ShapeDtypeStruct((3, CELLS, POINTS), F32),
        in_specs=[HBM] * 7,
        out_specs=pl.BlockSpec(memory_space=pltpu.VMEM),
        scratch_shapes=[
            pltpu.SMEM((2, LIST), jnp.int32),
            held[0],
            *held[2:],
            pltpu.SemaphoreType.DMA((7,)),
            pltpu.VMEM((GROUP // 2, 8, PW), F32),
            pltpu.VMEM((2, GROUP // 2, 8, RW), F32),
            pltpu.VMEM((6, 8, RW), F32),
            pltpu.VMEM((6, 8, RW), F32),
            pltpu.VMEM((CHUNKS, 2 * CHUNK, RW), F32),
            pltpu.VMEM((CHUNKS, 2 * CHUNK, RW), F32),
            pltpu.VMEM((CELLS + 1, 4, CHUNKS, CHUNK, LANES), F32),
            pltpu.VMEM((DEPTH, RW), BF16),
        ],
        compiler_params=pltpu.CompilerParams(vmem_limit_bytes=VMEM_BYTES),
        name="sums",
    )(table, halo, target, own, bend, up, weight)


def shards(surface, synthesis, analysis, stiffness, upsample, quad_weight, near_pairs, pair_count):
    outs = pl.pallas_call(
        exchange_kernel,
        out_shape=[jax.ShapeDtypeStruct(*h) for h in HANDED],
        in_specs=[HBM] * 8,
        out_specs=[HBM] * 7,
        scratch_shapes=[pltpu.VMEM(*h) for h in HANDED]
        + [
            pltpu.VMEM((LANES, LANES), F32),
            pltpu.VMEM((LANES, LANES), F32),
            pltpu.VMEM((LANES, LANES), F32),
            pltpu.VMEM((LANES, PW), F32),
            pltpu.VMEM((16, PW), F32),
            pltpu.VMEM((1, LANES), F32),
            pltpu.VMEM((3, CELLS, POINTS), F32),
            pltpu.VMEM((1, 1, 3, 1, SLOTS), jnp.int32),
            pltpu.VMEM((MODES, POINTS), F32),
            pltpu.VMEM((MODES, POINTS), F32),
            pltpu.VMEM((1, MODES), F32),
            pltpu.VMEM((POINTS, RAISED), F32),
            pltpu.VMEM((RAISED,), F32),
            pltpu.SMEM((1, 1, 1), jnp.int32),
            pltpu.SemaphoreType.DMA((8,)),
            pltpu.SemaphoreType.DMA((7,)),
            pltpu.SemaphoreType.DMA((27,)),
            pltpu.SemaphoreType.DMA((27,)),
        ],
        compiler_params=pltpu.CompilerParams(
            collective_id=0, has_side_effects=True, vmem_limit_bytes=VMEM_BYTES
        ),
        name="exchange",
    )(
        pair_count, jnp.swapaxes(surface[0, 0, 0], 0, 1), near_pairs.transpose(0, 1, 4, 2, 3),
        synthesis.T, analysis, stiffness[None, :], upsample.T, quad_weight,
    )
    velocity = sums(*outs)
    return jnp.swapaxes(velocity, 0, 1)[None, None, None]


def solution(mesh):
    return jax.shard_map(
        shards,
        mesh=mesh,
        in_specs=(
            P("tx", "ty", "tz", None, None, None),
            P(),
            P(),
            P(),
            P(),
            P(),
            P("tx", "ty", "tz", None, None),
            P("tx", "ty", "tz"),
        ),
        out_specs=P("tx", "ty", "tz", None, None, None),
        check_vma=False,
    )
```

```python
import functools
import math

import jax
import jax.numpy as jnp
from jax import lax
from jax.experimental import pallas as pl
from jax.experimental.pallas import tpu as pltpu
from jax.sharding import PartitionSpec as P

MESH = pl.DeviceIdType.MESH
F32 = jnp.float32
BF16 = jnp.bfloat16
smooth_sq = 0.25

CELLS = 4
POINTS = 312
RAISED = 1248
MODES = 169
SLOTS = 16
LANES = 128
PW = 384
RW = 1280
VMEM_BYTES = 63 * 2**20
OWN = 13
LIST = 512
CHUNKS = 3
CHUNK = POINTS // CHUNKS
GROUP = 32
DEPTH = 80


def split2(x):
    high = x.astype(BF16)
    return high, (x - high.astype(F32)).astype(BF16)


def split3(x):
    a = x.astype(BF16).astype(F32)
    rest = x - a
    b = rest.astype(BF16).astype(F32)
    return a, b, rest - b


def dot_nt(a, b):
    return lax.dot_general(a, b, (((1,), (1,)), ((), ())), preferred_element_type=F32)


def dot(a, b, precision=None):
    return jnp.dot(a, b, preferred_element_type=F32, precision=precision)


def split_rows(x):
    high, low = split2(x[:, :256])
    lane = lax.broadcasted_iota(jnp.int32, (x.shape[0], LANES), 1)
    rest = jnp.where(lane < 64, x[:, 256:], 0.0)
    rest_high = rest.astype(BF16).astype(F32)
    both = rest_high + pltpu.roll(rest - rest_high, 64, 1)
    return jnp.concatenate([high, low, high, both.astype(BF16), rest_high.astype(BF16)], axis=1)


def split_columns(place, x):
    width = x.shape[1]
    place[...] = jnp.zeros(place.shape, BF16)
    place[0:256, :width], place[256:512, :width] = split2(x[:256])
    rest = jnp.concatenate([x[256:], jnp.zeros((64 - (POINTS - 256), width), F32)], axis=0)
    high, low = split2(rest)
    place[512:576, :width] = high
    place[576:640, :width] = high
    place[640:704, :width] = low


def split_dot(x, place):
    whole = jnp.concatenate([place[0:256], place[0:256], place[256:512], place[512:768]], axis=0)
    return dot(x, whole)


def exchange_kernel(
    count_h, surface_h, pairs_h, synthesis_h, analysis_h, stiffness_h, upsample_h, weight_h,
    halo_h, table_h, target_h, own_h, bend_h, up_h, weight_out_h,
    halo, table, target, own_v, bend_v, up_v, weight,
    code_s, near_s, far_s, rows_s, own_s, slots_s,
    surface, pairs, synthesis, analysis, stiffness, upsample, weight_s, count,
    fetch_sem, store_sem, send_sem, recv_sem,
):
    sizes = [lax.axis_size(a) for a in ("tx", "ty", "tz")]
    here = [lax.axis_index(a) for a in ("tx", "ty", "tz")]
    others = [n for n in range(27) if n != OWN]

    def step(n):
        return (n // 9 - 1, n // 3 % 3 - 1, n % 3 - 1)

    def at(n):
        return tuple(lax.rem(h + d + s, s) for h, d, s in zip(here, step(n), sizes))

    def when_inside(n, act):
        inside = [
            jnp.logical_and(h + d >= 0, h + d < s)
            for h, d, s in zip(here, step(n), sizes) if d
        ]
        pl.when(functools.reduce(jnp.logical_and, inside))(act)

    def to(n):
        return pltpu.make_async_remote_copy(
            src_ref=halo.at[pl.ds(4 * OWN, CELLS)],
            dst_ref=halo.at[pl.ds(4 * (26 - n), CELLS)],
            send_sem=send_sem.at[n],
            recv_sem=recv_sem.at[26 - n],
            device_id=at(n),
            device_id_type=MESH,
        )

    fetches = []
    for i, (source, place) in enumerate((
        (surface_h, surface), (pairs_h, pairs), (count_h, count), (synthesis_h, synthesis),
        (analysis_h, analysis), (stiffness_h, stiffness), (upsample_h, upsample),
        (weight_h, weight_s),
    )):
        fetch = pltpu.make_async_copy(source, place, fetch_sem.at[i])
        fetch.start()
        fetches.append(fetch)
    barrier = pltpu.get_barrier_semaphore()
    halo[...] = jnp.full(halo.shape, -1.0, F32)
    for n in others:
        when_inside(n, lambda n=n: pl.semaphore_signal(
            barrier, inc=1, device_id=at(n), device_id_type=MESH
        ))

    own_s[...] = jnp.zeros((16, PW), F32)
    for fetch in fetches[:3]:
        fetch.wait()
    for c in range(CELLS):
        for k in range(3):
            own_s[4 * c + k : 4 * c + k + 1, :POINTS] = surface[k, c : c + 1, :]
    used = count[0, 0, 0]
    lane = lax.broadcasted_iota(jnp.int32, (1, LANES), 1)
    for c in range(CELLS):
        at_row = 4 * c
        halo[4 * OWN + c, 0:3] = own_s[at_row : at_row + 3, :LANES]
        halo[4 * OWN + c, 3:6] = own_s[at_row : at_row + 3, LANES : 2 * LANES]
        halo[4 * OWN + c, 6:7] = own_s[at_row : at_row + 1, 2 * LANES :] + pltpu.roll(
            own_s[at_row + 1 : at_row + 2, 2 * LANES :], 64, 1
        )
        row = own_s[at_row + 2 : at_row + 3, 2 * LANES :]
        if c < 3:
            slots_s[...] = jnp.full((1, LANES), -1.0, F32)
            slots_s[:, :SLOTS] = pairs[0, 0, c].astype(F32)
            pair = slots_s[...]
            if c == 1:
                pair = jnp.where(lane < used, pair, -1.0)
            pair = pltpu.roll(jnp.where(lane < SLOTS, pair, 0.0), 64, 1)
            row = row + pair
        halo[4 * OWN + c, 7:8] = row

    present = 1
    for h, s in zip(here, sizes):
        present = present * (1 + jnp.where(h > 0, 1, 0) + jnp.where(h < s - 1, 1, 0))
    pl.semaphore_wait(barrier, present - 1)
    for n in others:
        when_inside(n, lambda n=n: to(n).start())

    highest = lax.Precision.HIGHEST
    for fetch in fetches[3:]:
        fetch.wait()
    modes = analysis.shape[0]
    diagonal = lax.broadcasted_iota(jnp.int32, (modes, modes), 0) == lax.broadcasted_iota(
        jnp.int32, (modes, modes), 1
    )
    stiff = jnp.sum(jnp.where(diagonal, stiffness[...], 0.0), axis=1, keepdims=True)
    bend = lax.dot_general(
        analysis[...] * stiff, synthesis[...], (((0,), (0,)), ((), ())),
        preferred_element_type=F32, precision=highest,
    )
    split_columns(bend_v, bend)
    own = own_s[...]
    own_v[1, :, :POINTS] = dot(own[:, :POINTS], bend, highest)
    split_columns(up_v, upsample[...])
    own_v[0] = own
    weight[...] = jnp.ones((8, RW), F32)
    weight[4:8, :RAISED] = jnp.broadcast_to(weight_s[...][None, :] * (1.0 / math.sqrt(RAISED)), (4, RAISED))
    ones = jnp.ones((3, PW), F32)
    for c in range(CELLS):
        t = own[4 * c : 4 * c + 3, :]
        norm = jnp.sum(t * t, axis=0, keepdims=True) + smooth_sq
        t1, t2, t3 = split3(t)
        s1, s2, s3 = split3(norm)
        forms = []
        for kind in range(2):
            at_row = 4 * kind
            scale = 1.0 if kind else -2.0
            rows_s[...] = jnp.zeros((LANES, PW), F32)
            for block, part in enumerate((t1, t1, t2, t2, t1, t3)):
                rows_s[8 * block + at_row : 8 * block + at_row + 3, :] = part * scale
            for block in (6, 7, 8):
                rows_s[8 * block + at_row : 8 * block + at_row + 3, :] = -ones if kind else ones
            if not kind:
                rows_s[72:73, :] = s1
                rows_s[73:74, :] = s2
                rows_s[74:75, :] = s3
            forms.append(jnp.transpose(rows_s[...]))
        for q in range(CHUNKS):
            rows = slice(q * CHUNK, (q + 1) * CHUNK)
            target[c, q] = jnp.concatenate([forms[0][rows], forms[1][rows]], axis=0).astype(BF16)
    stores = []

    def store(place, out):
        copy = pltpu.make_async_copy(place, out, store_sem.at[len(stores)])
        copy.start()
        stores.append(copy)

    store(target, target_h)
    store(own_v, own_h)
    store(bend_v, bend_h)
    store(up_v, up_h)
    store(weight, weight_out_h)

    for n in others:
        when_inside(26 - n, lambda n=n: to(n).wait_recv())
    store(halo, halo_h)

    for ref, k in ((near_s, 0), (code_s, 1), (far_s, 2)):
        ref[...] = jnp.full((LANES, LANES), -1.0, F32)
        for n in range(27):
            ref[n : n + 1, :] = halo[4 * n + k, 7:8, :]
        ref[27:28, :] = halo[4 * OWN + k, 7:8, :]
    place = lax.broadcasted_iota(jnp.int32, (32, LANES), 0)
    place_f = place.astype(F32)
    lane32 = lax.broadcasted_iota(jnp.int32, (32, LANES), 1)
    code, near, far = code_s[:32, :], near_s[:32, :], far_s[:32, :]
    mask = jnp.logical_or(
        jnp.logical_and(place < 27, code == 26.0 - place_f),
        jnp.logical_and(place == 27, code >= 0.0),
    )
    mask = jnp.logical_and(mask, jnp.logical_and(lane32 >= 64, lane32 < 64 + SLOTS))
    value = jnp.where(
        place == 27, near * 128.0 + (code * 4.0 + far), far * 128.0 + (place_f * 4.0 + near)
    )
    taken = mask.astype(F32)
    upper = (
        lax.broadcasted_iota(jnp.int32, (LANES, LANES), 0)
        < lax.broadcasted_iota(jnp.int32, (LANES, LANES), 1)
    ).astype(F32)
    lower = (
        lax.broadcasted_iota(jnp.int32, (32, 32), 1) < lax.broadcasted_iota(jnp.int32, (32, 32), 0)
    ).astype(F32)
    per_row = jnp.broadcast_to(jnp.sum(taken, axis=1, keepdims=True), (32, LANES))
    before = jnp.dot(taken, upper, preferred_element_type=F32)
    above = jnp.dot(lower, per_row, preferred_element_type=F32)
    code_s[:32, :] = jnp.where(mask, before + above, -1.0)
    near_s[:32, :] = value
    spot = jnp.transpose(code_s[...])[64 : 64 + SLOTS]
    value = jnp.transpose(near_s[...])[64 : 64 + SLOTS]
    index = lax.broadcasted_iota(jnp.int32, (SLOTS, LIST), 1).astype(F32)
    listed = jnp.zeros((SLOTS, LIST), F32)
    for n in range(28):
        listed = listed + jnp.where(spot[:, n : n + 1] == index, value[:, n : n + 1], 0.0)
    table[0:1, :] = jnp.sum(listed, axis=0, keepdims=True).astype(jnp.int32)
    total = jnp.sum(jnp.sum(taken, axis=1, keepdims=True), axis=0, keepdims=True)
    table[1:2, :] = jnp.broadcast_to(total, (1, LIST)).astype(jnp.int32)

    store(table, table_h)
    for copy in stores:
        copy.wait()
    for n in others:
        when_inside(n, lambda n=n: to(n).wait_send())


def sums_kernel(
    table_h, halo_h, target_h, own_h, bend_h, up_h, weight_h,
    velocity,
    table, halo, target, own, bend, up, weight, fetch_sem,
    source_s, raised_s, wide0, wide1, forms0, forms1, total_s, operand_s,
):
    fetches = []
    for i, (source, place) in enumerate((
        (table_h, table), (halo_h, halo), (bend_h, bend), (up_h, up),
        (weight_h, weight), (target_h, target), (own_h, own),
    )):
        fetch = pltpu.make_async_copy(source, place, fetch_sem.at[i])
        fetch.start()
        fetches.append(fetch)
    wide_s, forms_s = (wide0, wide1), (forms0, forms1)
    total_s[...] = jnp.zeros(total_s.shape, F32)
    source_s[...] = jnp.zeros(source_s.shape, F32)
    for fetch in fetches:
        fetch.wait()
    count = table[1, 0]
    row8 = lax.broadcasted_iota(jnp.int32, (8, RW), 0)

    def group(g, carry):
        first = g * GROUP
        last = jnp.minimum(first + GROUP, count)

        for e in range(GROUP):
            tile = halo[table[0, first + e] % 128]
            at_row = e % 2 * 4
            source_s[e // 2, at_row : at_row + 3, :LANES] = tile[0:3]
            source_s[e // 2, at_row : at_row + 3, LANES : 2 * LANES] = tile[3:6]
            source_s[e // 2, at_row : at_row + 1, 2 * LANES :] = tile[6:7]
            source_s[e // 2, at_row + 1 : at_row + 2, 2 * LANES :] = pltpu.roll(tile[6:7], 64, 1)
            source_s[e // 2, at_row + 2 : at_row + 3, 2 * LANES :] = tile[7:8]
        places = split_rows(source_s[...].reshape(GROUP * 4, PW))
        bent = split_rows(split_dot(places, bend))
        raised = split_dot(jnp.concatenate([places, bent], axis=0), up)
        raised_s[...] = raised.reshape(2, GROUP // 2, 8, RW)

        def prepare(block, odd, slot):
            block = jnp.minimum(block, GROUP // 2 - 1)
            places, forces = raised_s[0, block], raised_s[1, block]
            if odd:
                places = pltpu.roll(places, 4, 0)
            else:
                forces = pltpu.roll(forces, 4, 0)
            both = jnp.where(row8 < 4, places, forces) * weight[...]
            for c in range(3):
                wide_s[slot][c] = jnp.broadcast_to(both[c : c + 1, :], (8, RW))
                wide_s[slot][3 + c] = jnp.broadcast_to(both[4 + c : 5 + c, :], (8, RW))
            p1, p2, p3 = split3(both)
            m1, m2, m3 = split3(both * jnp.where(row8 < 4, both, pltpu.roll(both, 4, 0)))
            operand_s[...] = jnp.concatenate(
                [p1, p2, p1, p2, p3, p1, m1, m2, m3, jnp.ones((8, RW), F32)], axis=0
            ).astype(BF16)

        def cell_of(e):
            return table[0, first + e] // 128

        def expand(cell, slot, q):
            forms_s[slot][q] = dot(target[cell, q][:, :DEPTH], operand_s[...])

        def fold(cell, slot, q, begin, size):
            acc = [None] * size
            for k in range(RW // LANES):
                ln = slice(k * LANES, (k + 1) * LANES)
                ys = [wide_s[slot][c, :, ln] for c in range(3)]
                gs = [wide_s[slot][3 + c, :, ln] for c in range(3)]
                for r in range(size):
                    row = 8 * (begin + r)
                    inverse = lax.rsqrt(forms_s[slot][q, row : row + 8, ln])
                    along = forms_s[slot][q, CHUNK + row : CHUNK + row + 8, ln]
                    factor = along * inverse * (inverse * inverse)
                    new = [gs[c] * inverse - ys[c] * factor for c in range(3)] + [factor]
                    acc[r] = new if k == 0 else [a + b for a, b in zip(acc[r], new)]
            for r in range(size):
                row = 8 * (begin + r)
                for c in range(4):
                    total_s[cell, c, q, row : row + 8, :] += acc[r][c]

        def two(i, carry):
            for half in range(2):
                e = 2 * i + half
                cell = jnp.where(e < last - first, cell_of(e), CELLS)
                later = cell_of(e + 1)
                prepare(i + half, 1 - half, 1 - half)

                def chunk(q, carry):
                    expand(later, 1 - half, q)
                    for begin in range(0, CHUNK // 8, 3):
                        fold(cell, half, q, begin, min(3, CHUNK // 8 - begin))
                    return carry

                lax.fori_loop(0, CHUNKS, chunk, 0)
            return carry

        prepare(0, 0, 0)
        for q in range(CHUNKS):
            expand(cell_of(0), 0, q)
        lax.fori_loop(0, (last - first + 1) // 2, two, 0)
        return carry

    lax.fori_loop(0, (count + GROUP - 1) // GROUP, group, 0)

    ones = jnp.ones((8, LANES), BF16)

    def reduced(x):
        high, low = split2(x)
        return (dot_nt(ones, high) + dot_nt(ones, low))[0:1, :]

    for c in range(CELLS):
        weight_sum = reduced(total_s[c, 3].reshape(POINTS, LANES))
        for k in range(3):
            row = 4 * c + k
            place = own[0, row : row + 1, :POINTS]
            velocity[k, c : c + 1, :] = (
                0.25 * own[1, row : row + 1, :POINTS]
                + reduced(total_s[c, k].reshape(POINTS, LANES))
                + place * weight_sum
            )


HBM = pl.BlockSpec(memory_space=pltpu.HBM)

HANDED = (
    ((27 * CELLS, 8, LANES), F32),
    ((2, LIST), jnp.int32),
    ((CELLS, CHUNKS, 2 * CHUNK, LANES), BF16),
    ((2, 16, PW), F32),
    ((768, PW), BF16),
    ((768, RW), BF16),
    ((8, RW), F32),
)


def sums(halo, table, target, own, bend, up, weight):
    held = [pltpu.VMEM(*h) for h in HANDED]
    return pl.pallas_call(
        sums_kernel,
        out_shape=jax.ShapeDtypeStruct((3, CELLS, POINTS), F32),
        in_specs=[HBM] * 7,
        out_specs=pl.BlockSpec(memory_space=pltpu.VMEM),
        scratch_shapes=[
            pltpu.SMEM((2, LIST), jnp.int32),
            held[0],
            *held[2:],
            pltpu.SemaphoreType.DMA((7,)),
            pltpu.VMEM((GROUP // 2, 8, PW), F32),
            pltpu.VMEM((2, GROUP // 2, 8, RW), F32),
            pltpu.VMEM((6, 8, RW), F32),
            pltpu.VMEM((6, 8, RW), F32),
            pltpu.VMEM((CHUNKS, 2 * CHUNK, RW), F32),
            pltpu.VMEM((CHUNKS, 2 * CHUNK, RW), F32),
            pltpu.VMEM((CELLS + 1, 4, CHUNKS, CHUNK, LANES), F32),
            pltpu.VMEM((DEPTH, RW), BF16),
        ],
        compiler_params=pltpu.CompilerParams(vmem_limit_bytes=VMEM_BYTES),
        name="sums",
    )(table, halo, target, own, bend, up, weight)


def shards(surface, synthesis, analysis, stiffness, upsample, quad_weight, near_pairs, pair_count):
    outs = pl.pallas_call(
        exchange_kernel,
        out_shape=[jax.ShapeDtypeStruct(*h) for h in HANDED],
        in_specs=[HBM] * 8,
        out_specs=[HBM] * 7,
        scratch_shapes=[pltpu.VMEM(*h) for h in HANDED]
        + [
            pltpu.VMEM((LANES, LANES), F32),
            pltpu.VMEM((LANES, LANES), F32),
            pltpu.VMEM((LANES, LANES), F32),
            pltpu.VMEM((LANES, PW), F32),
            pltpu.VMEM((16, PW), F32),
            pltpu.VMEM((1, LANES), F32),
            pltpu.VMEM((3, CELLS, POINTS), F32),
            pltpu.VMEM((1, 1, 3, 1, SLOTS), jnp.int32),
            pltpu.VMEM((MODES, POINTS), F32),
            pltpu.VMEM((MODES, POINTS), F32),
            pltpu.VMEM((1, MODES), F32),
            pltpu.VMEM((POINTS, RAISED), F32),
            pltpu.VMEM((RAISED,), F32),
            pltpu.SMEM((1, 1, 1), jnp.int32),
            pltpu.SemaphoreType.DMA((8,)),
            pltpu.SemaphoreType.DMA((7,)),
            pltpu.SemaphoreType.DMA((27,)),
            pltpu.SemaphoreType.DMA((27,)),
        ],
        compiler_params=pltpu.CompilerParams(
            collective_id=0, has_side_effects=True, vmem_limit_bytes=VMEM_BYTES
        ),
        name="exchange",
    )(
        pair_count, jnp.swapaxes(surface[0, 0, 0], 0, 1), near_pairs.transpose(0, 1, 4, 2, 3),
        synthesis.T, analysis, stiffness[None, :], upsample.T, quad_weight,
    )
    velocity = sums(*outs)
    return jnp.swapaxes(velocity, 0, 1)[None, None, None]


def solution(mesh):
    return jax.shard_map(
        shards,
        mesh=mesh,
        in_specs=(
            P("tx", "ty", "tz", None, None, None),
            P(),
            P(),
            P(),
            P(),
            P(),
            P("tx", "ty", "tz", None, None),
            P("tx", "ty", "tz"),
        ),
        out_specs=P("tx", "ty", "tz", None, None, None),
        check_vma=False,
    )
```

```python
import functools
import math

import jax
import jax.numpy as jnp
from jax import lax
from jax.experimental import pallas as pl
from jax.experimental.pallas import tpu as pltpu
from jax.sharding import PartitionSpec as P

MESH = pl.DeviceIdType.MESH
F32 = jnp.float32
BF16 = jnp.bfloat16
smooth_sq = 0.25

CELLS = 4
POINTS = 312
RAISED = 1248
MODES = 169
SLOTS = 16
LANES = 128
PW = 384
RW = 1280
VMEM_BYTES = 63 * 2**20
OWN = 13
LIST = 512
CHUNKS = 3
CHUNK = POINTS // CHUNKS
GROUP = 32
DEPTH = 80


def split2(x):
    high = x.astype(BF16)
    return high, (x - high.astype(F32)).astype(BF16)


def split3(x):
    a = x.astype(BF16).astype(F32)
    rest = x - a
    b = rest.astype(BF16).astype(F32)
    return a, b, rest - b


def dot_nt(a, b):
    return lax.dot_general(a, b, (((1,), (1,)), ((), ())), preferred_element_type=F32)


def dot(a, b, precision=None):
    return jnp.dot(a, b, preferred_element_type=F32, precision=precision)


def split_rows(x):
    high, low = split2(x[:, :256])
    lane = lax.broadcasted_iota(jnp.int32, (x.shape[0], LANES), 1)
    rest = jnp.where(lane < 64, x[:, 256:], 0.0)
    rest_high = rest.astype(BF16).astype(F32)
    both = rest_high + pltpu.roll(rest - rest_high, 64, 1)
    return jnp.concatenate([high, low, high, both.astype(BF16), rest_high.astype(BF16)], axis=1)


def split_columns(place, x):
    width = x.shape[1]
    place[...] = jnp.zeros(place.shape, BF16)
    place[0:256, :width], place[256:512, :width] = split2(x[:256])
    rest = jnp.concatenate([x[256:], jnp.zeros((64 - (POINTS - 256), width), F32)], axis=0)
    high, low = split2(rest)
    place[512:576, :width] = high
    place[576:640, :width] = high
    place[640:704, :width] = low


def split_dot(x, place):
    whole = jnp.concatenate([place[0:256], place[0:256], place[256:512], place[512:768]], axis=0)
    return dot(x, whole)


def exchange_kernel(
    count_h, surface_h, pairs_h, synthesis_h, analysis_h, stiffness_h, upsample_h, weight_h,
    halo_h, table_h, target_h, own_h, bend_h, up_h, weight_out_h,
    halo, table, target, own_v, bend_v, up_v, weight,
    code_s, near_s, far_s, rows_s, own_s, slots_s,
    surface, pairs, synthesis, analysis, stiffness, upsample, weight_s, count,
    fetch_sem, store_sem, send_sem, recv_sem,
):
    sizes = [lax.axis_size(a) for a in ("tx", "ty", "tz")]
    here = [lax.axis_index(a) for a in ("tx", "ty", "tz")]
    others = [n for n in range(27) if n != OWN]

    def step(n):
        return (n // 9 - 1, n // 3 % 3 - 1, n % 3 - 1)

    def at(n):
        return tuple(lax.rem(h + d + s, s) for h, d, s in zip(here, step(n), sizes))

    def when_inside(n, act):
        inside = [
            jnp.logical_and(h + d >= 0, h + d < s)
            for h, d, s in zip(here, step(n), sizes) if d
        ]
        pl.when(functools.reduce(jnp.logical_and, inside))(act)

    def to(n):
        return pltpu.make_async_remote_copy(
            src_ref=halo.at[pl.ds(4 * OWN, CELLS)],
            dst_ref=halo.at[pl.ds(4 * (26 - n), CELLS)],
            send_sem=send_sem.at[n],
            recv_sem=recv_sem.at[26 - n],
            device_id=at(n),
            device_id_type=MESH,
        )

    fetches = []
    for i, (source, place) in enumerate((
        (surface_h, surface), (pairs_h, pairs), (count_h, count), (synthesis_h, synthesis),
        (analysis_h, analysis), (stiffness_h, stiffness), (upsample_h, upsample),
        (weight_h, weight_s),
    )):
        fetch = pltpu.make_async_copy(source, place, fetch_sem.at[i])
        fetch.start()
        fetches.append(fetch)
    barrier = pltpu.get_barrier_semaphore()
    halo[...] = jnp.full(halo.shape, -1.0, F32)
    for n in others:
        when_inside(n, lambda n=n: pl.semaphore_signal(
            barrier, inc=1, device_id=at(n), device_id_type=MESH
        ))

    own_s[...] = jnp.zeros((16, PW), F32)
    for fetch in fetches[:3]:
        fetch.wait()
    for c in range(CELLS):
        for k in range(3):
            own_s[4 * c + k : 4 * c + k + 1, :POINTS] = surface[k, c : c + 1, :]
    used = count[0, 0, 0]
    lane = lax.broadcasted_iota(jnp.int32, (1, LANES), 1)
    for c in range(CELLS):
        at_row = 4 * c
        halo[4 * OWN + c, 0:3] = own_s[at_row : at_row + 3, :LANES]
        halo[4 * OWN + c, 3:6] = own_s[at_row : at_row + 3, LANES : 2 * LANES]
        halo[4 * OWN + c, 6:7] = own_s[at_row : at_row + 1, 2 * LANES :] + pltpu.roll(
            own_s[at_row + 1 : at_row + 2, 2 * LANES :], 64, 1
        )
        row = own_s[at_row + 2 : at_row + 3, 2 * LANES :]
        if c < 3:
            slots_s[...] = jnp.full((1, LANES), -1.0, F32)
            slots_s[:, :SLOTS] = pairs[0, 0, c].astype(F32)
            pair = slots_s[...]
            if c == 1:
                pair = jnp.where(lane < used, pair, -1.0)
            pair = pltpu.roll(jnp.where(lane < SLOTS, pair, 0.0), 64, 1)
            row = row + pair
        halo[4 * OWN + c, 7:8] = row

    present = 1
    for h, s in zip(here, sizes):
        present = present * (1 + jnp.where(h > 0, 1, 0) + jnp.where(h < s - 1, 1, 0))
    pl.semaphore_wait(barrier, present - 1)
    for n in others:
        when_inside(n, lambda n=n: to(n).start())

    highest = lax.Precision.HIGHEST
    for fetch in fetches[3:]:
        fetch.wait()
    modes = analysis.shape[0]
    diagonal = lax.broadcasted_iota(jnp.int32, (modes, modes), 0) == lax.broadcasted_iota(
        jnp.int32, (modes, modes), 1
    )
    stiff = jnp.sum(jnp.where(diagonal, stiffness[...], 0.0), axis=1, keepdims=True)
    bend = lax.dot_general(
        analysis[...] * stiff, synthesis[...], (((0,), (0,)), ((), ())),
        preferred_element_type=F32, precision=highest,
    )
    split_columns(bend_v, bend)
    own = own_s[...]
    own_v[1, :, :POINTS] = dot(own[:, :POINTS], bend, highest)
    split_columns(up_v, upsample[...])
    own_v[0] = own
    weight[...] = jnp.ones((8, RW), F32)
    weight[4:8, :RAISED] = jnp.broadcast_to(weight_s[...][None, :] * (1.0 / math.sqrt(RAISED)), (4, RAISED))
    ones = jnp.ones((3, PW), F32)
    for c in range(CELLS):
        t = own[4 * c : 4 * c + 3, :]
        norm = jnp.sum(t * t, axis=0, keepdims=True) + smooth_sq
        t1, t2, t3 = split3(t)
        s1, s2, s3 = split3(norm)
        forms = []
        for kind in range(2):
            at_row = 4 * kind
            scale = 1.0 if kind else -2.0
            rows_s[...] = jnp.zeros((LANES, PW), F32)
            for block, part in enumerate((t1, t1, t2, t2, t1, t3)):
                rows_s[8 * block + at_row : 8 * block + at_row + 3, :] = part * scale
            for block in (6, 7, 8):
                rows_s[8 * block + at_row : 8 * block + at_row + 3, :] = -ones if kind else ones
            if not kind:
                rows_s[72:73, :] = s1
                rows_s[73:74, :] = s2
                rows_s[74:75, :] = s3
            forms.append(jnp.transpose(rows_s[...]))
        for q in range(CHUNKS):
            rows = slice(q * CHUNK, (q + 1) * CHUNK)
            target[c, q] = jnp.concatenate([forms[0][rows], forms[1][rows]], axis=0).astype(BF16)
    stores = []

    def store(place, out):
        copy = pltpu.make_async_copy(place, out, store_sem.at[len(stores)])
        copy.start()
        stores.append(copy)

    store(target, target_h)
    store(own_v, own_h)
    store(bend_v, bend_h)
    store(up_v, up_h)
    store(weight, weight_out_h)

    for n in others:
        when_inside(26 - n, lambda n=n: to(n).wait_recv())
    store(halo, halo_h)

    for ref, k in ((near_s, 0), (code_s, 1), (far_s, 2)):
        ref[...] = jnp.full((LANES, LANES), -1.0, F32)
        for n in range(27):
            ref[n : n + 1, :] = halo[4 * n + k, 7:8, :]
        ref[27:28, :] = halo[4 * OWN + k, 7:8, :]
    place = lax.broadcasted_iota(jnp.int32, (32, LANES), 0)
    place_f = place.astype(F32)
    lane32 = lax.broadcasted_iota(jnp.int32, (32, LANES), 1)
    code, near, far = code_s[:32, :], near_s[:32, :], far_s[:32, :]
    mask = jnp.logical_or(
        jnp.logical_and(place < 27, code == 26.0 - place_f),
        jnp.logical_and(place == 27, code >= 0.0),
    )
    mask = jnp.logical_and(mask, jnp.logical_and(lane32 >= 64, lane32 < 64 + SLOTS))
    value = jnp.where(
        place == 27, near * 128.0 + (code * 4.0 + far), far * 128.0 + (place_f * 4.0 + near)
    )
    taken = mask.astype(F32)
    upper = (
        lax.broadcasted_iota(jnp.int32, (LANES, LANES), 0)
        < lax.broadcasted_iota(jnp.int32, (LANES, LANES), 1)
    ).astype(F32)
    lower = (
        lax.broadcasted_iota(jnp.int32, (32, 32), 1) < lax.broadcasted_iota(jnp.int32, (32, 32), 0)
    ).astype(F32)
    per_row = jnp.broadcast_to(jnp.sum(taken, axis=1, keepdims=True), (32, LANES))
    before = jnp.dot(taken, upper, preferred_element_type=F32)
    above = jnp.dot(lower, per_row, preferred_element_type=F32)
    code_s[:32, :] = jnp.where(mask, before + above, -1.0)
    near_s[:32, :] = value
    spot = jnp.transpose(code_s[...])[64 : 64 + SLOTS]
    value = jnp.transpose(near_s[...])[64 : 64 + SLOTS]
    index = lax.broadcasted_iota(jnp.int32, (SLOTS, LIST), 1).astype(F32)
    listed = jnp.zeros((SLOTS, LIST), F32)
    for n in range(28):
        listed = listed + jnp.where(spot[:, n : n + 1] == index, value[:, n : n + 1], 0.0)
    table[0:1, :] = jnp.sum(listed, axis=0, keepdims=True).astype(jnp.int32)
    total = jnp.sum(jnp.sum(taken, axis=1, keepdims=True), axis=0, keepdims=True)
    table[1:2, :] = jnp.broadcast_to(total, (1, LIST)).astype(jnp.int32)

    store(table, table_h)
    for copy in stores:
        copy.wait()
    for n in others:
        when_inside(n, lambda n=n: to(n).wait_send())


def sums_kernel(
    table_h, halo_h, target_h, own_h, bend_h, up_h, weight_h,
    velocity,
    table, halo, target, own, bend, up, weight, fetch_sem,
    source_s, raised_s, wide0, wide1, forms0, forms1, total_s, operand_s,
):
    fetches = []
    for i, (source, place) in enumerate((
        (table_h, table), (halo_h, halo), (bend_h, bend), (up_h, up),
        (weight_h, weight), (target_h, target), (own_h, own),
    )):
        fetch = pltpu.make_async_copy(source, place, fetch_sem.at[i])
        fetch.start()
        fetches.append(fetch)
    wide_s, forms_s = (wide0, wide1), (forms0, forms1)
    total_s[...] = jnp.zeros(total_s.shape, F32)
    source_s[...] = jnp.zeros(source_s.shape, F32)
    fetches[0].wait()
    fetches[1].wait()
    count = table[1, 0]
    row8 = lax.broadcasted_iota(jnp.int32, (8, RW), 0)

    def arrive(g, *which):
        def wait():
            for i in which:
                fetches[i].wait()

        pl.when(g == 0)(wait)

    def group(g, carry):
        first = g * GROUP
        last = jnp.minimum(first + GROUP, count)

        for e in range(GROUP):
            tile = halo[table[0, first + e] % 128]
            at_row = e % 2 * 4
            source_s[e // 2, at_row : at_row + 3, :LANES] = tile[0:3]
            source_s[e // 2, at_row : at_row + 3, LANES : 2 * LANES] = tile[3:6]
            source_s[e // 2, at_row : at_row + 1, 2 * LANES :] = tile[6:7]
            source_s[e // 2, at_row + 1 : at_row + 2, 2 * LANES :] = pltpu.roll(tile[6:7], 64, 1)
            source_s[e // 2, at_row + 2 : at_row + 3, 2 * LANES :] = tile[7:8]
        arrive(g, 2)
        places = split_rows(source_s[...].reshape(GROUP * 4, PW))
        bent = split_rows(split_dot(places, bend))
        arrive(g, 3, 4, 5)
        raised = split_dot(jnp.concatenate([places, bent], axis=0), up)
        raised_s[...] = raised.reshape(2, GROUP // 2, 8, RW)

        def prepare(block, odd, slot):
            block = jnp.minimum(block, GROUP // 2 - 1)
            places, forces = raised_s[0, block], raised_s[1, block]
            if odd:
                places = pltpu.roll(places, 4, 0)
            else:
                forces = pltpu.roll(forces, 4, 0)
            both = jnp.where(row8 < 4, places, forces) * weight[...]
            for c in range(3):
                wide_s[slot][c] = jnp.broadcast_to(both[c : c + 1, :], (8, RW))
                wide_s[slot][3 + c] = jnp.broadcast_to(both[4 + c : 5 + c, :], (8, RW))
            p1, p2, p3 = split3(both)
            m1, m2, m3 = split3(both * jnp.where(row8 < 4, both, pltpu.roll(both, 4, 0)))
            operand_s[...] = jnp.concatenate(
                [p1, p2, p1, p2, p3, p1, m1, m2, m3, jnp.ones((8, RW), F32)], axis=0
            ).astype(BF16)

        def cell_of(e):
            return table[0, first + e] // 128

        def expand(cell, slot, q):
            forms_s[slot][q] = dot(target[cell, q][:, :DEPTH], operand_s[...])

        def fold(cell, slot, q, begin, size):
            acc = [None] * size
            for k in range(RW // LANES):
                ln = slice(k * LANES, (k + 1) * LANES)
                ys = [wide_s[slot][c, :, ln] for c in range(3)]
                gs = [wide_s[slot][3 + c, :, ln] for c in range(3)]
                for r in range(size):
                    row = 8 * (begin + r)
                    inverse = lax.rsqrt(forms_s[slot][q, row : row + 8, ln])
                    along = forms_s[slot][q, CHUNK + row : CHUNK + row + 8, ln]
                    factor = along * inverse * (inverse * inverse)
                    new = [gs[c] * inverse - ys[c] * factor for c in range(3)] + [factor]
                    acc[r] = new if k == 0 else [a + b for a, b in zip(acc[r], new)]
            for r in range(size):
                row = 8 * (begin + r)
                for c in range(4):
                    total_s[cell, c, q, row : row + 8, :] += acc[r][c]

        def two(i, carry):
            for half in range(2):
                e = 2 * i + half
                cell = cell_of(e)
                turns = jnp.where(e < last - first, CHUNKS, 0) if half else CHUNKS
                later = cell_of(e + 1)
                prepare(i + half, 1 - half, 1 - half)

                def chunk(q, carry):
                    expand(later, 1 - half, q)
                    for begin in range(0, CHUNK // 8, 3):
                        fold(cell, half, q, begin, min(3, CHUNK // 8 - begin))
                    return carry

                lax.fori_loop(0, turns, chunk, 0)
            return carry

        prepare(0, 0, 0)
        for q in range(CHUNKS):
            expand(cell_of(0), 0, q)
        lax.fori_loop(0, (last - first + 1) // 2, two, 0)
        return carry

    lax.fori_loop(0, (count + GROUP - 1) // GROUP, group, 0)

    fetches[6].wait()
    ones = jnp.ones((8, 2 * LANES), BF16)
    for c in range(CELLS):
        split = jnp.concatenate(split2(total_s[c].reshape(4 * POINTS, LANES)), axis=1)
        summed = dot_nt(ones, split)[0:1, :]
        parts = [summed[:, k * POINTS : (k + 1) * POINTS] for k in range(4)]
        for k in range(3):
            row = 4 * c + k
            velocity[k, c : c + 1, :] = (
                0.25 * own[1, row : row + 1, :POINTS]
                + parts[k]
                + own[0, row : row + 1, :POINTS] * parts[3]
            )


HBM = pl.BlockSpec(memory_space=pltpu.HBM)

HANDED = (
    ((27 * CELLS, 8, LANES), F32),
    ((2, LIST), jnp.int32),
    ((CELLS, CHUNKS, 2 * CHUNK, LANES), BF16),
    ((2, 16, PW), F32),
    ((768, PW), BF16),
    ((768, RW), BF16),
    ((8, RW), F32),
)


def sums(halo, table, target, own, bend, up, weight):
    held = [pltpu.VMEM(*h) for h in HANDED]
    return pl.pallas_call(
        sums_kernel,
        out_shape=jax.ShapeDtypeStruct((3, CELLS, POINTS), F32),
        in_specs=[HBM] * 7,
        out_specs=pl.BlockSpec(memory_space=pltpu.VMEM),
        scratch_shapes=[
            pltpu.SMEM((2, LIST), jnp.int32),
            held[0],
            *held[2:],
            pltpu.SemaphoreType.DMA((7,)),
            pltpu.VMEM((GROUP // 2, 8, PW), F32),
            pltpu.VMEM((2, GROUP // 2, 8, RW), F32),
            pltpu.VMEM((6, 8, RW), F32),
            pltpu.VMEM((6, 8, RW), F32),
            pltpu.VMEM((CHUNKS, 2 * CHUNK, RW), F32),
            pltpu.VMEM((CHUNKS, 2 * CHUNK, RW), F32),
            pltpu.VMEM((CELLS, 4, CHUNKS, CHUNK, LANES), F32),
            pltpu.VMEM((DEPTH, RW), BF16),
        ],
        compiler_params=pltpu.CompilerParams(vmem_limit_bytes=VMEM_BYTES),
        name="sums",
    )(table, halo, target, own, bend, up, weight)


def shards(surface, synthesis, analysis, stiffness, upsample, quad_weight, near_pairs, pair_count):
    outs = pl.pallas_call(
        exchange_kernel,
        out_shape=[jax.ShapeDtypeStruct(*h) for h in HANDED],
        in_specs=[HBM] * 8,
        out_specs=[HBM] * 7,
        scratch_shapes=[pltpu.VMEM(*h) for h in HANDED]
        + [
            pltpu.VMEM((LANES, LANES), F32),
            pltpu.VMEM((LANES, LANES), F32),
            pltpu.VMEM((LANES, LANES), F32),
            pltpu.VMEM((LANES, PW), F32),
            pltpu.VMEM((16, PW), F32),
            pltpu.VMEM((1, LANES), F32),
            pltpu.VMEM((3, CELLS, POINTS), F32),
            pltpu.VMEM((1, 1, 3, 1, SLOTS), jnp.int32),
            pltpu.VMEM((MODES, POINTS), F32),
            pltpu.VMEM((MODES, POINTS), F32),
            pltpu.VMEM((1, MODES), F32),
            pltpu.VMEM((POINTS, RAISED), F32),
            pltpu.VMEM((RAISED,), F32),
            pltpu.SMEM((1, 1, 1), jnp.int32),
            pltpu.SemaphoreType.DMA((8,)),
            pltpu.SemaphoreType.DMA((7,)),
            pltpu.SemaphoreType.DMA((27,)),
            pltpu.SemaphoreType.DMA((27,)),
        ],
        compiler_params=pltpu.CompilerParams(
            collective_id=0, has_side_effects=True, vmem_limit_bytes=VMEM_BYTES
        ),
        name="exchange",
    )(
        pair_count, jnp.swapaxes(surface[0, 0, 0], 0, 1), near_pairs.transpose(0, 1, 4, 2, 3),
        synthesis.T, analysis, stiffness[None, :], upsample.T, quad_weight,
    )
    velocity = sums(*outs)
    return jnp.swapaxes(velocity, 0, 1)[None, None, None]


def solution(mesh):
    return jax.shard_map(
        shards,
        mesh=mesh,
        in_specs=(
            P("tx", "ty", "tz", None, None, None),
            P(),
            P(),
            P(),
            P(),
            P(),
            P("tx", "ty", "tz", None, None),
            P("tx", "ty", "tz"),
        ),
        out_specs=P("tx", "ty", "tz", None, None, None),
        check_vma=False,
    )
```

```python
import functools
import math

import jax
import jax.numpy as jnp
from jax import lax
from jax.experimental import pallas as pl
from jax.experimental.pallas import tpu as pltpu
from jax.sharding import PartitionSpec as P

MESH = pl.DeviceIdType.MESH
F32 = jnp.float32
BF16 = jnp.bfloat16
smooth_sq = 0.25

CELLS = 4
POINTS = 312
RAISED = 1248
MODES = 169
SLOTS = 16
LANES = 128
PW = 384
RW = 1280
VMEM_BYTES = 48 * 2**20
OWN = 13
LIST = 512
CHUNKS = 3
CHUNK = POINTS // CHUNKS
GROUP = 32
DEPTH = 80


def split2(x):
    high = x.astype(BF16)
    return high, (x - high.astype(F32)).astype(BF16)


def split3(x):
    a = x.astype(BF16).astype(F32)
    rest = x - a
    b = rest.astype(BF16).astype(F32)
    return a, b, rest - b


def dot_nt(a, b):
    return lax.dot_general(a, b, (((1,), (1,)), ((), ())), preferred_element_type=F32)


def dot(a, b, precision=None):
    return jnp.dot(a, b, preferred_element_type=F32, precision=precision)


def split_rows(x):
    high, low = split2(x[:, :256])
    lane = lax.broadcasted_iota(jnp.int32, (x.shape[0], LANES), 1)
    rest = jnp.where(lane < 64, x[:, 256:], 0.0)
    rest_high = rest.astype(BF16).astype(F32)
    both = rest_high + pltpu.roll(rest - rest_high, 64, 1)
    return jnp.concatenate([high, low, high, both.astype(BF16), rest_high.astype(BF16)], axis=1)


def split_columns(place, x):
    width = x.shape[1]
    place[...] = jnp.zeros(place.shape, BF16)
    place[0:256, :width], place[256:512, :width] = split2(x[:256])
    rest = jnp.concatenate([x[256:], jnp.zeros((64 - (POINTS - 256), width), F32)], axis=0)
    high, low = split2(rest)
    place[512:576, :width] = high
    place[576:640, :width] = high
    place[640:704, :width] = low


def split_dot(x, place):
    whole = jnp.concatenate([place[0:256], place[0:256], place[256:512], place[512:768]], axis=0)
    return dot(x, whole)


def exchange_kernel(
    count_h, surface_h, pairs_h, synthesis_h, analysis_h, stiffness_h, upsample_h, weight_h,
    halo, table, target, own_v, bend_v, up_v, weight,
    code_s, near_s, far_s, rows_s, own_s, slots_s,
    surface, pairs, synthesis, analysis, stiffness, upsample, weight_s, count,
    fetch_sem, send_sem, recv_sem,
):
    sizes = [lax.axis_size(a) for a in ("tx", "ty", "tz")]
    here = [lax.axis_index(a) for a in ("tx", "ty", "tz")]
    others = [n for n in range(27) if n != OWN]

    def step(n):
        return (n // 9 - 1, n // 3 % 3 - 1, n % 3 - 1)

    def at(n):
        return tuple(lax.rem(h + d + s, s) for h, d, s in zip(here, step(n), sizes))

    def when_inside(n, act):
        inside = [
            jnp.logical_and(h + d >= 0, h + d < s)
            for h, d, s in zip(here, step(n), sizes) if d
        ]
        pl.when(functools.reduce(jnp.logical_and, inside))(act)

    def to(n):
        return pltpu.make_async_remote_copy(
            src_ref=halo.at[pl.ds(4 * OWN, CELLS)],
            dst_ref=halo.at[pl.ds(4 * (26 - n), CELLS)],
            send_sem=send_sem.at[n],
            recv_sem=recv_sem.at[26 - n],
            device_id=at(n),
            device_id_type=MESH,
        )

    fetches = []
    for i, (source, place) in enumerate((
        (surface_h, surface), (pairs_h, pairs), (count_h, count), (synthesis_h, synthesis),
        (analysis_h, analysis), (stiffness_h, stiffness), (upsample_h, upsample),
        (weight_h, weight_s),
    )):
        fetch = pltpu.make_async_copy(source, place, fetch_sem.at[i])
        fetch.start()
        fetches.append(fetch)
    barrier = pltpu.get_barrier_semaphore()
    halo[...] = jnp.full(halo.shape, -1.0, F32)
    for n in others:
        when_inside(n, lambda n=n: pl.semaphore_signal(
            barrier, inc=1, device_id=at(n), device_id_type=MESH
        ))

    own_s[...] = jnp.zeros((16, PW), F32)
    for fetch in fetches[:3]:
        fetch.wait()
    for c in range(CELLS):
        for k in range(3):
            own_s[4 * c + k : 4 * c + k + 1, :POINTS] = surface[k, c : c + 1, :]
    used = count[0, 0, 0]
    lane = lax.broadcasted_iota(jnp.int32, (1, LANES), 1)
    for c in range(CELLS):
        at_row = 4 * c
        halo[4 * OWN + c, 0:3] = own_s[at_row : at_row + 3, :LANES]
        halo[4 * OWN + c, 3:6] = own_s[at_row : at_row + 3, LANES : 2 * LANES]
        halo[4 * OWN + c, 6:7] = own_s[at_row : at_row + 1, 2 * LANES :] + pltpu.roll(
            own_s[at_row + 1 : at_row + 2, 2 * LANES :], 64, 1
        )
        row = own_s[at_row + 2 : at_row + 3, 2 * LANES :]
        if c < 3:
            slots_s[...] = jnp.full((1, LANES), -1.0, F32)
            slots_s[:, :SLOTS] = pairs[0, 0, c].astype(F32)
            pair = slots_s[...]
            if c == 1:
                pair = jnp.where(lane < used, pair, -1.0)
            pair = pltpu.roll(jnp.where(lane < SLOTS, pair, 0.0), 64, 1)
            row = row + pair
        halo[4 * OWN + c, 7:8] = row

    present = 1
    for h, s in zip(here, sizes):
        present = present * (1 + jnp.where(h > 0, 1, 0) + jnp.where(h < s - 1, 1, 0))
    pl.semaphore_wait(barrier, present - 1)
    for n in others:
        when_inside(n, lambda n=n: to(n).start())

    highest = lax.Precision.HIGHEST
    for fetch in fetches[3:]:
        fetch.wait()
    modes = analysis.shape[0]
    diagonal = lax.broadcasted_iota(jnp.int32, (modes, modes), 0) == lax.broadcasted_iota(
        jnp.int32, (modes, modes), 1
    )
    stiff = jnp.sum(jnp.where(diagonal, stiffness[...], 0.0), axis=1, keepdims=True)
    bend = lax.dot_general(
        analysis[...] * stiff, synthesis[...], (((0,), (0,)), ((), ())),
        preferred_element_type=F32, precision=highest,
    )
    split_columns(bend_v, bend)
    own = own_s[...]
    own_v[1, :, :POINTS] = dot(own[:, :POINTS], bend, highest)
    split_columns(up_v, upsample[...])
    own_v[0] = own
    weight[...] = jnp.ones((8, RW), F32)
    weight[4:8, :RAISED] = jnp.broadcast_to(weight_s[...][None, :] * (1.0 / math.sqrt(RAISED)), (4, RAISED))
    ones = jnp.ones((3, PW), F32)
    for c in range(CELLS):
        t = own[4 * c : 4 * c + 3, :]
        norm = jnp.sum(t * t, axis=0, keepdims=True) + smooth_sq
        t1, t2, t3 = split3(t)
        s1, s2, s3 = split3(norm)
        forms = []
        for kind in range(2):
            at_row = 4 * kind
            scale = 1.0 if kind else -2.0
            rows_s[...] = jnp.zeros((LANES, PW), F32)
            for block, part in enumerate((t1, t1, t2, t2, t1, t3)):
                rows_s[8 * block + at_row : 8 * block + at_row + 3, :] = part * scale
            for block in (6, 7, 8):
                rows_s[8 * block + at_row : 8 * block + at_row + 3, :] = -ones if kind else ones
            if not kind:
                rows_s[72:73, :] = s1
                rows_s[73:74, :] = s2
                rows_s[74:75, :] = s3
            forms.append(jnp.transpose(rows_s[...]))
        for q in range(CHUNKS):
            rows = slice(q * CHUNK, (q + 1) * CHUNK)
            target[c, q] = jnp.concatenate([forms[0][rows], forms[1][rows]], axis=0).astype(BF16)

    for n in others:
        when_inside(26 - n, lambda n=n: to(n).wait_recv())

    for ref, k in ((near_s, 0), (code_s, 1), (far_s, 2)):
        ref[...] = jnp.full((LANES, LANES), -1.0, F32)
        for n in range(27):
            ref[n : n + 1, :] = halo[4 * n + k, 7:8, :]
        ref[27:28, :] = halo[4 * OWN + k, 7:8, :]
    place = lax.broadcasted_iota(jnp.int32, (32, LANES), 0)
    place_f = place.astype(F32)
    lane32 = lax.broadcasted_iota(jnp.int32, (32, LANES), 1)
    code, near, far = code_s[:32, :], near_s[:32, :], far_s[:32, :]
    mask = jnp.logical_or(
        jnp.logical_and(place < 27, code == 26.0 - place_f),
        jnp.logical_and(place == 27, code >= 0.0),
    )
    mask = jnp.logical_and(mask, jnp.logical_and(lane32 >= 64, lane32 < 64 + SLOTS))
    value = jnp.where(
        place == 27, near * 128.0 + (code * 4.0 + far), far * 128.0 + (place_f * 4.0 + near)
    )
    taken = mask.astype(F32)
    upper = (
        lax.broadcasted_iota(jnp.int32, (LANES, LANES), 0)
        < lax.broadcasted_iota(jnp.int32, (LANES, LANES), 1)
    ).astype(F32)
    lower = (
        lax.broadcasted_iota(jnp.int32, (32, 32), 1) < lax.broadcasted_iota(jnp.int32, (32, 32), 0)
    ).astype(F32)
    per_row = jnp.broadcast_to(jnp.sum(taken, axis=1, keepdims=True), (32, LANES))
    before = jnp.dot(taken, upper, preferred_element_type=F32)
    above = jnp.dot(lower, per_row, preferred_element_type=F32)
    code_s[:32, :] = jnp.where(mask, before + above, -1.0)
    near_s[:32, :] = value
    spot = jnp.transpose(code_s[...])[64 : 64 + SLOTS]
    value = jnp.transpose(near_s[...])[64 : 64 + SLOTS]
    index = lax.broadcasted_iota(jnp.int32, (SLOTS, LIST), 1).astype(F32)
    listed = jnp.zeros((SLOTS, LIST), F32)
    for n in range(28):
        listed = listed + jnp.where(spot[:, n : n + 1] == index, value[:, n : n + 1], 0.0)
    table[0:1, :] = jnp.sum(listed, axis=0, keepdims=True).astype(jnp.int32)
    total = jnp.sum(jnp.sum(taken, axis=1, keepdims=True), axis=0, keepdims=True)
    table[1:2, :] = jnp.broadcast_to(total, (1, LIST)).astype(jnp.int32)

    for n in others:
        when_inside(n, lambda n=n: to(n).wait_send())


def sums_kernel(
    table, halo, target, own, bend, up, weight,
    velocity,
    source_s, raised_s, wide0, wide1, forms0, forms1, total_s, operand_s,
):
    wide_s, forms_s = (wide0, wide1), (forms0, forms1)
    total_s[...] = jnp.zeros(total_s.shape, F32)
    source_s[...] = jnp.zeros(source_s.shape, F32)
    count = table[1, 0]
    row8 = lax.broadcasted_iota(jnp.int32, (8, RW), 0)

    def group(g, carry):
        first = g * GROUP
        last = jnp.minimum(first + GROUP, count)

        for e in range(GROUP):
            tile = halo[table[0, first + e] % 128]
            at_row = e % 2 * 4
            source_s[e // 2, at_row : at_row + 3, :LANES] = tile[0:3]
            source_s[e // 2, at_row : at_row + 3, LANES : 2 * LANES] = tile[3:6]
            source_s[e // 2, at_row : at_row + 1, 2 * LANES :] = tile[6:7]
            source_s[e // 2, at_row + 1 : at_row + 2, 2 * LANES :] = pltpu.roll(tile[6:7], 64, 1)
            source_s[e // 2, at_row + 2 : at_row + 3, 2 * LANES :] = tile[7:8]
        places = split_rows(source_s[...].reshape(GROUP * 4, PW))
        bent = split_rows(split_dot(places, bend))
        raised = split_dot(jnp.concatenate([places, bent], axis=0), up)
        raised_s[...] = raised.reshape(2, GROUP // 2, 8, RW)

        def prepare(block, odd, slot):
            block = jnp.minimum(block, GROUP // 2 - 1)
            places, forces = raised_s[0, block], raised_s[1, block]
            if odd:
                places = pltpu.roll(places, 4, 0)
            else:
                forces = pltpu.roll(forces, 4, 0)
            both = jnp.where(row8 < 4, places, forces) * weight[...]
            for c in range(3):
                wide_s[slot][c] = jnp.broadcast_to(both[c : c + 1, :], (8, RW))
                wide_s[slot][3 + c] = jnp.broadcast_to(both[4 + c : 5 + c, :], (8, RW))
            p1, p2, p3 = split3(both)
            m1, m2, m3 = split3(both * jnp.where(row8 < 4, both, pltpu.roll(both, 4, 0)))
            operand_s[...] = jnp.concatenate(
                [p1, p2, p1, p2, p3, p1, m1, m2, m3, jnp.ones((8, RW), F32)], axis=0
            ).astype(BF16)

        def cell_of(e):
            return table[0, first + e] // 128

        def expand(cell, slot, q):
            forms_s[slot][q] = dot(target[cell, q][:, :DEPTH], operand_s[...])

        def fold(cell, slot, q, begin, size):
            acc = [None] * size
            for k in range(RW // LANES):
                ln = slice(k * LANES, (k + 1) * LANES)
                ys = [wide_s[slot][c, :, ln] for c in range(3)]
                gs = [wide_s[slot][3 + c, :, ln] for c in range(3)]
                for r in range(size):
                    row = 8 * (begin + r)
                    inverse = lax.rsqrt(forms_s[slot][q, row : row + 8, ln])
                    along = forms_s[slot][q, CHUNK + row : CHUNK + row + 8, ln]
                    factor = along * inverse * (inverse * inverse)
                    new = [gs[c] * inverse - ys[c] * factor for c in range(3)] + [factor]
                    acc[r] = new if k == 0 else [a + b for a, b in zip(acc[r], new)]
            for r in range(size):
                row = 8 * (begin + r)
                for c in range(4):
                    total_s[cell, c, q, row : row + 8, :] += acc[r][c]

        def two(i, carry):
            for half in range(2):
                e = 2 * i + half
                cell = cell_of(e)
                turns = jnp.where(e < last - first, CHUNKS, 0) if half else CHUNKS
                later = cell_of(e + 1)
                prepare(i + half, 1 - half, 1 - half)

                def chunk(q, carry):
                    expand(later, 1 - half, q)
                    for begin in range(0, CHUNK // 8, 3):
                        fold(cell, half, q, begin, min(3, CHUNK // 8 - begin))
                    return carry

                lax.fori_loop(0, turns, chunk, 0)
            return carry

        prepare(0, 0, 0)
        for q in range(CHUNKS):
            expand(cell_of(0), 0, q)
        lax.fori_loop(0, (last - first + 1) // 2, two, 0)
        return carry

    lax.fori_loop(0, (count + GROUP - 1) // GROUP, group, 0)

    ones = jnp.ones((8, 2 * LANES), BF16)
    for c in range(CELLS):
        split = jnp.concatenate(split2(total_s[c].reshape(4 * POINTS, LANES)), axis=1)
        summed = dot_nt(ones, split)[0:1, :]
        parts = [summed[:, k * POINTS : (k + 1) * POINTS] for k in range(4)]
        for k in range(3):
            row = 4 * c + k
            velocity[k, c : c + 1, :] = (
                0.25 * own[1, row : row + 1, :POINTS]
                + parts[k]
                + own[0, row : row + 1, :POINTS] * parts[3]
            )


HBM = pl.BlockSpec(memory_space=pltpu.HBM)
VMEM = pl.BlockSpec(memory_space=pltpu.VMEM)
SMEM = pl.BlockSpec(memory_space=pltpu.SMEM)

HANDED = (
    ((27 * CELLS, 8, LANES), F32),
    ((2, LIST), jnp.int32),
    ((CELLS, CHUNKS, 2 * CHUNK, LANES), BF16),
    ((2, 16, PW), F32),
    ((768, PW), BF16),
    ((768, RW), BF16),
    ((8, RW), F32),
)


def sums(halo, table, target, own, bend, up, weight):
    return pl.pallas_call(
        sums_kernel,
        out_shape=jax.ShapeDtypeStruct((3, CELLS, POINTS), F32),
        in_specs=[SMEM] + [VMEM] * 6,
        out_specs=VMEM,
        scratch_shapes=[
            pltpu.VMEM((GROUP // 2, 8, PW), F32),
            pltpu.VMEM((2, GROUP // 2, 8, RW), F32),
            pltpu.VMEM((6, 8, RW), F32),
            pltpu.VMEM((6, 8, RW), F32),
            pltpu.VMEM((CHUNKS, 2 * CHUNK, RW), F32),
            pltpu.VMEM((CHUNKS, 2 * CHUNK, RW), F32),
            pltpu.VMEM((CELLS, 4, CHUNKS, CHUNK, LANES), F32),
            pltpu.VMEM((DEPTH, RW), BF16),
        ],
        compiler_params=pltpu.CompilerParams(vmem_limit_bytes=VMEM_BYTES),
        name="sums",
    )(table, halo, target, own, bend, up, weight)


def shards(surface, synthesis, analysis, stiffness, upsample, quad_weight, near_pairs, pair_count):
    outs = pl.pallas_call(
        exchange_kernel,
        out_shape=[jax.ShapeDtypeStruct(*h) for h in HANDED],
        in_specs=[HBM] * 8,
        out_specs=[VMEM] * 7,
        scratch_shapes=[
            pltpu.VMEM((LANES, LANES), F32),
            pltpu.VMEM((LANES, LANES), F32),
            pltpu.VMEM((LANES, LANES), F32),
            pltpu.VMEM((LANES, PW), F32),
            pltpu.VMEM((16, PW), F32),
            pltpu.VMEM((1, LANES), F32),
            pltpu.VMEM((3, CELLS, POINTS), F32),
            pltpu.VMEM((1, 1, 3, 1, SLOTS), jnp.int32),
            pltpu.VMEM((MODES, POINTS), F32),
            pltpu.VMEM((MODES, POINTS), F32),
            pltpu.VMEM((1, MODES), F32),
            pltpu.VMEM((POINTS, RAISED), F32),
            pltpu.VMEM((RAISED,), F32),
            pltpu.SMEM((1, 1, 1), jnp.int32),
            pltpu.SemaphoreType.DMA((8,)),
            pltpu.SemaphoreType.DMA((27,)),
            pltpu.SemaphoreType.DMA((27,)),
        ],
        compiler_params=pltpu.CompilerParams(
            collective_id=0, has_side_effects=True, vmem_limit_bytes=VMEM_BYTES
        ),
        name="exchange",
    )(pair_count, *[
        pltpu.with_memory_space_constraint(x, pltpu.HBM)
        for x in (
            jnp.swapaxes(surface[0, 0, 0], 0, 1),
            near_pairs.transpose(0, 1, 4, 2, 3), synthesis.T, analysis, stiffness[None, :],
            upsample.T, quad_weight,
        )
    ])
    velocity = sums(*outs)
    return jnp.swapaxes(velocity, 0, 1)[None, None, None]


def solution(mesh):
    return jax.shard_map(
        shards,
        mesh=mesh,
        in_specs=(
            P("tx", "ty", "tz", None, None, None),
            P(),
            P(),
            P(),
            P(),
            P(),
            P("tx", "ty", "tz", None, None),
            P("tx", "ty", "tz"),
        ),
        out_specs=P("tx", "ty", "tz", None, None, None),
        check_vma=False,
    )
```

```python
import functools
import math

import jax
import jax.numpy as jnp
from jax import lax
from jax.experimental import pallas as pl
from jax.experimental.pallas import tpu as pltpu
from jax.sharding import PartitionSpec as P

MESH = pl.DeviceIdType.MESH
F32 = jnp.float32
BF16 = jnp.bfloat16
smooth_sq = 0.25

CELLS = 4
POINTS = 312
RAISED = 1248
MODES = 169
SLOTS = 16
LANES = 128
PW = 384
RW = 1280
VMEM_BYTES = 48 * 2**20
OWN = 13
LIST = 512
CHUNKS = 3
CHUNK = POINTS // CHUNKS
GROUP = 32
DEPTH = 80


def split2(x):
    high = x.astype(BF16)
    return high, (x - high.astype(F32)).astype(BF16)


def split3(x):
    a = x.astype(BF16).astype(F32)
    rest = x - a
    b = rest.astype(BF16).astype(F32)
    return a, b, rest - b


def dot_nt(a, b):
    return lax.dot_general(a, b, (((1,), (1,)), ((), ())), preferred_element_type=F32)


def dot(a, b, precision=None):
    return jnp.dot(a, b, preferred_element_type=F32, precision=precision)


def split_rows(x):
    high, low = split2(x[:, :256])
    lane = lax.broadcasted_iota(jnp.int32, (x.shape[0], LANES), 1)
    rest = jnp.where(lane < 64, x[:, 256:], 0.0)
    rest_high = rest.astype(BF16).astype(F32)
    both = rest_high + pltpu.roll(rest - rest_high, 64, 1)
    return jnp.concatenate([high, low, high, both.astype(BF16), rest_high.astype(BF16)], axis=1)


def split_columns(place, x):
    width = x.shape[1]
    place[...] = jnp.zeros(place.shape, BF16)
    place[0:256, :width], place[256:512, :width] = split2(x[:256])
    rest = jnp.concatenate([x[256:], jnp.zeros((64 - (POINTS - 256), width), F32)], axis=0)
    high, low = split2(rest)
    place[512:576, :width] = high
    place[576:640, :width] = high
    place[640:704, :width] = low


def split_dot(x, place):
    whole = jnp.concatenate([place[0:256], place[0:256], place[256:512], place[512:768]], axis=0)
    return dot(x, whole)


def exchange_kernel(
    count_h, surface_h, pairs_h, synthesis_h, analysis_h, stiffness_h, upsample_h, weight_h,
    halo, table, target, own_v, bend_v, up_v, weight,
    code_s, near_s, far_s, rows_s, own_s, slots_s,
    surface, pairs, synthesis, analysis, stiffness, upsample, weight_s, count,
    fetch_sem, send_sem, recv_sem,
):
    sizes = [lax.axis_size(a) for a in ("tx", "ty", "tz")]
    here = [lax.axis_index(a) for a in ("tx", "ty", "tz")]
    others = [n for n in range(27) if n != OWN]

    def step(n):
        return (n // 9 - 1, n // 3 % 3 - 1, n % 3 - 1)

    def at(n):
        return tuple(h + d for h, d in zip(here, step(n)))

    def when_inside(n, act):
        inside = [
            jnp.logical_and(h + d >= 0, h + d < s)
            for h, d, s in zip(here, step(n), sizes) if d
        ]
        pl.when(functools.reduce(jnp.logical_and, inside))(act)

    def to(n):
        return pltpu.make_async_remote_copy(
            src_ref=halo.at[pl.ds(4 * OWN, CELLS)],
            dst_ref=halo.at[pl.ds(4 * (26 - n), CELLS)],
            send_sem=send_sem.at[n],
            recv_sem=recv_sem.at[26 - n],
            device_id=at(n),
            device_id_type=MESH,
        )

    fetches = []
    for i, (source, place) in enumerate((
        (surface_h, surface), (pairs_h, pairs), (count_h, count), (synthesis_h, synthesis),
        (analysis_h, analysis), (stiffness_h, stiffness), (upsample_h, upsample),
        (weight_h, weight_s),
    )):
        fetch = pltpu.make_async_copy(source, place, fetch_sem.at[i])
        fetch.start()
        fetches.append(fetch)
    barrier = pltpu.get_barrier_semaphore()
    halo[...] = jnp.full(halo.shape, -1.0, F32)
    for n in others:
        when_inside(n, lambda n=n: pl.semaphore_signal(
            barrier, inc=1, device_id=at(n), device_id_type=MESH
        ))

    own_s[...] = jnp.zeros((16, PW), F32)
    for fetch in fetches[:3]:
        fetch.wait()
    for c in range(CELLS):
        for k in range(3):
            own_s[4 * c + k : 4 * c + k + 1, :POINTS] = surface[k, c : c + 1, :]
    used = count[0, 0, 0]
    lane = lax.broadcasted_iota(jnp.int32, (1, LANES), 1)
    for c in range(CELLS):
        at_row = 4 * c
        halo[4 * OWN + c, 0:3] = own_s[at_row : at_row + 3, :LANES]
        halo[4 * OWN + c, 3:6] = own_s[at_row : at_row + 3, LANES : 2 * LANES]
        halo[4 * OWN + c, 6:7] = own_s[at_row : at_row + 1, 2 * LANES :] + pltpu.roll(
            own_s[at_row + 1 : at_row + 2, 2 * LANES :], 64, 1
        )
        row = own_s[at_row + 2 : at_row + 3, 2 * LANES :]
        if c < 3:
            slots_s[...] = jnp.full((1, LANES), -1.0, F32)
            slots_s[:, :SLOTS] = pairs[0, 0, c].astype(F32)
            pair = slots_s[...]
            if c == 1:
                pair = jnp.where(lane < used, pair, -1.0)
            pair = pltpu.roll(jnp.where(lane < SLOTS, pair, 0.0), 64, 1)
            row = row + pair
        halo[4 * OWN + c, 7:8] = row

    present = 1
    for h, s in zip(here, sizes):
        present = present * (1 + jnp.where(h > 0, 1, 0) + jnp.where(h < s - 1, 1, 0))
    pl.semaphore_wait(barrier, present - 1)
    for n in others:
        when_inside(n, lambda n=n: to(n).start())

    highest = lax.Precision.HIGHEST
    for fetch in fetches[3:]:
        fetch.wait()
    modes = analysis.shape[0]
    diagonal = lax.broadcasted_iota(jnp.int32, (modes, modes), 0) == lax.broadcasted_iota(
        jnp.int32, (modes, modes), 1
    )
    stiff = jnp.sum(jnp.where(diagonal, stiffness[...], 0.0), axis=1, keepdims=True)
    bend = lax.dot_general(
        analysis[...] * stiff, synthesis[...], (((0,), (0,)), ((), ())),
        preferred_element_type=F32, precision=highest,
    )
    split_columns(bend_v, bend)
    own = own_s[...]
    own_v[1, :, :POINTS] = dot(own[:, :POINTS], bend, highest)
    split_columns(up_v, upsample[...])
    own_v[0] = own
    weight[...] = jnp.ones((8, RW), F32)
    weight[4:8, :RAISED] = jnp.broadcast_to(weight_s[...][None, :] * (1.0 / math.sqrt(RAISED)), (4, RAISED))
    ones = jnp.ones((3, PW), F32)
    for c in range(CELLS):
        t = own[4 * c : 4 * c + 3, :]
        norm = jnp.sum(t * t, axis=0, keepdims=True) + smooth_sq
        t1, t2, t3 = split3(t)
        s1, s2, s3 = split3(norm)
        forms = []
        for kind in range(2):
            at_row = 4 * kind
            scale = 1.0 if kind else -2.0
            rows_s[...] = jnp.zeros((LANES, PW), F32)
            for block, part in enumerate((t1, t1, t2, t2, t1, t3)):
                rows_s[8 * block + at_row : 8 * block + at_row + 3, :] = part * scale
            for block in (6, 7, 8):
                rows_s[8 * block + at_row : 8 * block + at_row + 3, :] = -ones if kind else ones
            if not kind:
                rows_s[72:73, :] = s1
                rows_s[73:74, :] = s2
                rows_s[74:75, :] = s3
            forms.append(jnp.transpose(rows_s[...]))
        for q in range(CHUNKS):
            rows = slice(q * CHUNK, (q + 1) * CHUNK)
            target[c, q] = jnp.concatenate([forms[0][rows], forms[1][rows]], axis=0).astype(BF16)

    for n in others:
        when_inside(26 - n, lambda n=n: to(n).wait_recv())

    for ref, k in ((near_s, 0), (code_s, 1), (far_s, 2)):
        ref[...] = jnp.full((LANES, LANES), -1.0, F32)
        for n in range(27):
            ref[n : n + 1, :] = halo[4 * n + k, 7:8, :]
        ref[27:28, :] = halo[4 * OWN + k, 7:8, :]
    place = lax.broadcasted_iota(jnp.int32, (32, LANES), 0)
    place_f = place.astype(F32)
    lane32 = lax.broadcasted_iota(jnp.int32, (32, LANES), 1)
    code, near, far = code_s[:32, :], near_s[:32, :], far_s[:32, :]
    mask = jnp.logical_or(
        jnp.logical_and(place < 27, code == 26.0 - place_f),
        jnp.logical_and(place == 27, code >= 0.0),
    )
    mask = jnp.logical_and(mask, jnp.logical_and(lane32 >= 64, lane32 < 64 + SLOTS))
    value = jnp.where(
        place == 27, near * 128.0 + (code * 4.0 + far), far * 128.0 + (place_f * 4.0 + near)
    )
    taken = mask.astype(F32)
    upper = (
        lax.broadcasted_iota(jnp.int32, (LANES, LANES), 0)
        < lax.broadcasted_iota(jnp.int32, (LANES, LANES), 1)
    ).astype(F32)
    lower = (
        lax.broadcasted_iota(jnp.int32, (32, 32), 1) < lax.broadcasted_iota(jnp.int32, (32, 32), 0)
    ).astype(F32)
    per_row = jnp.broadcast_to(jnp.sum(taken, axis=1, keepdims=True), (32, LANES))
    before = jnp.dot(taken, upper, preferred_element_type=F32)
    above = jnp.dot(lower, per_row, preferred_element_type=F32)
    code_s[:32, :] = jnp.where(mask, before + above, -1.0)
    near_s[:32, :] = value
    spot = jnp.transpose(code_s[...])[64 : 64 + SLOTS]
    value = jnp.transpose(near_s[...])[64 : 64 + SLOTS]
    index = lax.broadcasted_iota(jnp.int32, (SLOTS, LIST), 1).astype(F32)
    listed = jnp.zeros((SLOTS, LIST), F32)
    for n in range(28):
        listed = listed + jnp.where(spot[:, n : n + 1] == index, value[:, n : n + 1], 0.0)
    table[0:1, :] = jnp.sum(listed, axis=0, keepdims=True).astype(jnp.int32)
    total = jnp.sum(jnp.sum(taken, axis=1, keepdims=True), axis=0, keepdims=True)
    table[1:2, :] = jnp.broadcast_to(total, (1, LIST)).astype(jnp.int32)

    for n in others:
        when_inside(n, lambda n=n: to(n).wait_send())


def sums_kernel(
    table, halo, target, own, bend, up, weight,
    velocity,
    source_s, raised_s, wide0, wide1, forms0, forms1, total_s, operand_s,
):
    wide_s, forms_s = (wide0, wide1), (forms0, forms1)
    total_s[...] = jnp.zeros(total_s.shape, F32)
    source_s[...] = jnp.zeros(source_s.shape, F32)
    count = table[1, 0]
    row8 = lax.broadcasted_iota(jnp.int32, (8, RW), 0)

    def group(g, carry):
        first = g * GROUP
        last = jnp.minimum(first + GROUP, count)

        for e in range(GROUP):
            tile = halo[table[0, first + e] % 128]
            at_row = e % 2 * 4
            source_s[e // 2, at_row : at_row + 3, :LANES] = tile[0:3]
            source_s[e // 2, at_row : at_row + 3, LANES : 2 * LANES] = tile[3:6]
            source_s[e // 2, at_row : at_row + 1, 2 * LANES :] = tile[6:7]
            source_s[e // 2, at_row + 1 : at_row + 2, 2 * LANES :] = pltpu.roll(tile[6:7], 64, 1)
            source_s[e // 2, at_row + 2 : at_row + 3, 2 * LANES :] = tile[7:8]
        places = split_rows(source_s[...].reshape(GROUP * 4, PW))
        bent = split_rows(split_dot(places, bend))
        raised = split_dot(jnp.concatenate([places, bent], axis=0), up)
        raised_s[...] = raised.reshape(2, GROUP // 2, 8, RW)

        def prepare(block, odd, slot):
            block = jnp.minimum(block, GROUP // 2 - 1)
            places, forces = raised_s[0, block], raised_s[1, block]
            if odd:
                places = pltpu.roll(places, 4, 0)
            else:
                forces = pltpu.roll(forces, 4, 0)
            both = jnp.where(row8 < 4, places, forces) * weight[...]
            for c in range(3):
                wide_s[slot][c] = jnp.broadcast_to(both[c : c + 1, :], (8, RW))
                wide_s[slot][3 + c] = jnp.broadcast_to(both[4 + c : 5 + c, :], (8, RW))
            p1, p2, p3 = split3(both)
            m1, m2, m3 = split3(both * jnp.where(row8 < 4, both, pltpu.roll(both, 4, 0)))
            operand_s[...] = jnp.concatenate(
                [p1, p2, p1, p2, p3, p1, m1, m2, m3, jnp.ones((8, RW), F32)], axis=0
            ).astype(BF16)

        def cell_of(e):
            return table[0, first + e] // 128

        def expand(cell, slot, q):
            forms_s[slot][q] = dot(target[cell, q][:, :DEPTH], operand_s[...])

        def fold(cell, slot, q, begin, size):
            acc = [None] * size
            for k in range(RW // LANES):
                ln = slice(k * LANES, (k + 1) * LANES)
                ys = [wide_s[slot][c, :, ln] for c in range(3)]
                gs = [wide_s[slot][3 + c, :, ln] for c in range(3)]
                for r in range(size):
                    row = 8 * (begin + r)
                    inverse = lax.rsqrt(forms_s[slot][q, row : row + 8, ln])
                    along = forms_s[slot][q, CHUNK + row : CHUNK + row + 8, ln]
                    factor = along * inverse * (inverse * inverse)
                    new = [gs[c] * inverse - ys[c] * factor for c in range(3)] + [factor]
                    acc[r] = new if k == 0 else [a + b for a, b in zip(acc[r], new)]
            for r in range(size):
                row = 8 * (begin + r)
                for c in range(4):
                    total_s[cell, c, q, row : row + 8, :] += acc[r][c]

        def two(i, carry):
            for half in range(2):
                e = 2 * i + half
                cell = cell_of(e)
                turns = jnp.where(e < last - first, CHUNKS, 0) if half else CHUNKS
                later = cell_of(e + 1)
                prepare(i + half, 1 - half, 1 - half)

                def chunk(q, carry):
                    expand(later, 1 - half, q)
                    for begin in range(0, CHUNK // 8, 3):
                        fold(cell, half, q, begin, min(3, CHUNK // 8 - begin))
                    return carry

                lax.fori_loop(0, turns, chunk, 0)
            return carry

        prepare(0, 0, 0)
        for q in range(CHUNKS):
            expand(cell_of(0), 0, q)
        lax.fori_loop(0, (last - first + 1) // 2, two, 0)
        return carry

    lax.fori_loop(0, (count + GROUP - 1) // GROUP, group, 0)

    ones = jnp.ones((8, 2 * LANES), BF16)
    for c in range(CELLS):
        split = jnp.concatenate(split2(total_s[c].reshape(4 * POINTS, LANES)), axis=1)
        summed = dot_nt(ones, split)[0:1, :]
        parts = [summed[:, k * POINTS : (k + 1) * POINTS] for k in range(4)]
        for k in range(3):
            row = 4 * c + k
            velocity[k, c : c + 1, :] = (
                0.25 * own[1, row : row + 1, :POINTS]
                + parts[k]
                + own[0, row : row + 1, :POINTS] * parts[3]
            )


HBM = pl.BlockSpec(memory_space=pltpu.HBM)
VMEM = pl.BlockSpec(memory_space=pltpu.VMEM)
SMEM = pl.BlockSpec(memory_space=pltpu.SMEM)

HANDED = (
    ((27 * CELLS, 8, LANES), F32),
    ((2, LIST), jnp.int32),
    ((CELLS, CHUNKS, 2 * CHUNK, LANES), BF16),
    ((2, 16, PW), F32),
    ((768, PW), BF16),
    ((768, RW), BF16),
    ((8, RW), F32),
)


def sums(halo, table, target, own, bend, up, weight):
    return pl.pallas_call(
        sums_kernel,
        out_shape=jax.ShapeDtypeStruct((3, CELLS, POINTS), F32),
        in_specs=[SMEM] + [VMEM] * 6,
        out_specs=VMEM,
        scratch_shapes=[
            pltpu.VMEM((GROUP // 2, 8, PW), F32),
            pltpu.VMEM((2, GROUP // 2, 8, RW), F32),
            pltpu.VMEM((6, 8, RW), F32),
            pltpu.VMEM((6, 8, RW), F32),
            pltpu.VMEM((CHUNKS, 2 * CHUNK, RW), F32),
            pltpu.VMEM((CHUNKS, 2 * CHUNK, RW), F32),
            pltpu.VMEM((CELLS, 4, CHUNKS, CHUNK, LANES), F32),
            pltpu.VMEM((DEPTH, RW), BF16),
        ],
        compiler_params=pltpu.CompilerParams(vmem_limit_bytes=VMEM_BYTES),
        name="sums",
    )(table, halo, target, own, bend, up, weight)


def shards(surface, synthesis, analysis, stiffness, upsample, quad_weight, near_pairs, pair_count):
    outs = pl.pallas_call(
        exchange_kernel,
        out_shape=[jax.ShapeDtypeStruct(*h) for h in HANDED],
        in_specs=[HBM] * 8,
        out_specs=[VMEM] * 7,
        scratch_shapes=[
            pltpu.VMEM((LANES, LANES), F32),
            pltpu.VMEM((LANES, LANES), F32),
            pltpu.VMEM((LANES, LANES), F32),
            pltpu.VMEM((LANES, PW), F32),
            pltpu.VMEM((16, PW), F32),
            pltpu.VMEM((1, LANES), F32),
            pltpu.VMEM((3, CELLS, POINTS), F32),
            pltpu.VMEM((1, 1, 3, 1, SLOTS), jnp.int32),
            pltpu.VMEM((MODES, POINTS), F32),
            pltpu.VMEM((MODES, POINTS), F32),
            pltpu.VMEM((1, MODES), F32),
            pltpu.VMEM((POINTS, RAISED), F32),
            pltpu.VMEM((RAISED,), F32),
            pltpu.SMEM((1, 1, 1), jnp.int32),
            pltpu.SemaphoreType.DMA((8,)),
            pltpu.SemaphoreType.DMA((27,)),
            pltpu.SemaphoreType.DMA((27,)),
        ],
        compiler_params=pltpu.CompilerParams(
            collective_id=0, has_side_effects=True, vmem_limit_bytes=VMEM_BYTES
        ),
        name="exchange",
    )(pair_count, *[
        pltpu.with_memory_space_constraint(x, pltpu.HBM)
        for x in (
            jnp.swapaxes(surface[0, 0, 0], 0, 1),
            near_pairs.transpose(0, 1, 4, 2, 3), synthesis.T, analysis, stiffness[None, :],
            upsample.T, quad_weight,
        )
    ])
    velocity = sums(*outs)
    return jnp.swapaxes(velocity, 0, 1)[None, None, None]


def solution(mesh):
    return jax.shard_map(
        shards,
        mesh=mesh,
        in_specs=(
            P("tx", "ty", "tz", None, None, None),
            P(),
            P(),
            P(),
            P(),
            P(),
            P("tx", "ty", "tz", None, None),
            P("tx", "ty", "tz"),
        ),
        out_specs=P("tx", "ty", "tz", None, None, None),
        check_vma=False,
    )
```

```python
import functools
import math

import jax
import jax.numpy as jnp
from jax import lax
from jax.experimental import pallas as pl
from jax.experimental.pallas import tpu as pltpu
from jax.sharding import PartitionSpec as P

MESH = pl.DeviceIdType.MESH
F32 = jnp.float32
BF16 = jnp.bfloat16
smooth_sq = 0.25

CELLS = 4
POINTS = 312
RAISED = 1248
MODES = 169
SLOTS = 16
LANES = 128
PW = 384
RW = 1280
VMEM_BYTES = 48 * 2**20
OWN = 13
LIST = 512
CHUNKS = 3
CHUNK = POINTS // CHUNKS
GROUP = 40
DEPTH = 80


def split2(x):
    high = x.astype(BF16)
    return high, (x - high.astype(F32)).astype(BF16)


def split3(x):
    a = x.astype(BF16).astype(F32)
    rest = x - a
    b = rest.astype(BF16).astype(F32)
    return a, b, rest - b


def dot_nt(a, b):
    return lax.dot_general(a, b, (((1,), (1,)), ((), ())), preferred_element_type=F32)


def dot(a, b, precision=None):
    return jnp.dot(a, b, preferred_element_type=F32, precision=precision)


def split_rows(x):
    high, low = split2(x[:, :256])
    lane = lax.broadcasted_iota(jnp.int32, (x.shape[0], LANES), 1)
    rest = jnp.where(lane < 64, x[:, 256:], 0.0)
    rest_high = rest.astype(BF16).astype(F32)
    both = rest_high + pltpu.roll(rest - rest_high, 64, 1)
    return jnp.concatenate([high, low, high, both.astype(BF16), rest_high.astype(BF16)], axis=1)


def split_columns(place, x):
    width = x.shape[1]
    place[...] = jnp.zeros(place.shape, BF16)
    place[0:256, :width], place[256:512, :width] = split2(x[:256])
    rest = jnp.concatenate([x[256:], jnp.zeros((64 - (POINTS - 256), width), F32)], axis=0)
    high, low = split2(rest)
    place[512:576, :width] = high
    place[576:640, :width] = high
    place[640:704, :width] = low


def split_dot(x, place):
    whole = jnp.concatenate([place[0:256], place[0:256], place[256:512], place[512:768]], axis=0)
    return dot(x, whole)


def exchange_kernel(
    count_h, surface_h, pairs_h, synthesis_h, analysis_h, stiffness_h, upsample_h, weight_h,
    halo, table, target, own_v, bend_v, up_v, weight,
    code_s, near_s, far_s, rows_s, own_s, slots_s,
    surface, pairs, synthesis, analysis, stiffness, upsample, weight_s, count,
    fetch_sem, send_sem, recv_sem,
):
    sizes = [lax.axis_size(a) for a in ("tx", "ty", "tz")]
    here = [lax.axis_index(a) for a in ("tx", "ty", "tz")]
    others = [n for n in range(27) if n != OWN]

    def step(n):
        return (n // 9 - 1, n // 3 % 3 - 1, n % 3 - 1)

    def at(n):
        return tuple(lax.rem(h + d + s, s) for h, d, s in zip(here, step(n), sizes))

    def when_inside(n, act):
        inside = [
            jnp.logical_and(h + d >= 0, h + d < s)
            for h, d, s in zip(here, step(n), sizes) if d
        ]
        pl.when(functools.reduce(jnp.logical_and, inside))(act)

    def to(n):
        return pltpu.make_async_remote_copy(
            src_ref=halo.at[pl.ds(4 * OWN, CELLS)],
            dst_ref=halo.at[pl.ds(4 * (26 - n), CELLS)],
            send_sem=send_sem.at[n],
            recv_sem=recv_sem.at[26 - n],
            device_id=at(n),
            device_id_type=MESH,
        )

    fetches = []
    for i, (source, place) in enumerate((
        (surface_h, surface), (pairs_h, pairs), (count_h, count), (synthesis_h, synthesis),
        (analysis_h, analysis), (stiffness_h, stiffness), (upsample_h, upsample),
        (weight_h, weight_s),
    )):
        fetch = pltpu.make_async_copy(source, place, fetch_sem.at[i])
        fetch.start()
        fetches.append(fetch)
    barrier = pltpu.get_barrier_semaphore()
    halo[...] = jnp.full(halo.shape, -1.0, F32)
    for n in others:
        when_inside(n, lambda n=n: pl.semaphore_signal(
            barrier, inc=1, device_id=at(n), device_id_type=MESH
        ))

    own_s[...] = jnp.zeros((16, PW), F32)
    for fetch in fetches[:3]:
        fetch.wait()
    for c in range(CELLS):
        for k in range(3):
            own_s[4 * c + k : 4 * c + k + 1, :POINTS] = surface[k, c : c + 1, :]
    used = count[0, 0, 0]
    lane = lax.broadcasted_iota(jnp.int32, (1, LANES), 1)
    for c in range(CELLS):
        at_row = 4 * c
        halo[4 * OWN + c, 0:3] = own_s[at_row : at_row + 3, :LANES]
        halo[4 * OWN + c, 3:6] = own_s[at_row : at_row + 3, LANES : 2 * LANES]
        halo[4 * OWN + c, 6:7] = own_s[at_row : at_row + 1, 2 * LANES :] + pltpu.roll(
            own_s[at_row + 1 : at_row + 2, 2 * LANES :], 64, 1
        )
        row = own_s[at_row + 2 : at_row + 3, 2 * LANES :]
        if c < 3:
            slots_s[...] = jnp.full((1, LANES), -1.0, F32)
            slots_s[:, :SLOTS] = pairs[0, 0, c].astype(F32)
            pair = slots_s[...]
            if c == 1:
                pair = jnp.where(lane < used, pair, -1.0)
            pair = pltpu.roll(jnp.where(lane < SLOTS, pair, 0.0), 64, 1)
            row = row + pair
        halo[4 * OWN + c, 7:8] = row

    present = 1
    for h, s in zip(here, sizes):
        present = present * (1 + jnp.where(h > 0, 1, 0) + jnp.where(h < s - 1, 1, 0))
    pl.semaphore_wait(barrier, present - 1)
    for n in others:
        when_inside(n, lambda n=n: to(n).start())

    highest = lax.Precision.HIGHEST
    for fetch in fetches[3:]:
        fetch.wait()
    modes = analysis.shape[0]
    diagonal = lax.broadcasted_iota(jnp.int32, (modes, modes), 0) == lax.broadcasted_iota(
        jnp.int32, (modes, modes), 1
    )
    stiff = jnp.sum(jnp.where(diagonal, stiffness[...], 0.0), axis=1, keepdims=True)
    bend = lax.dot_general(
        analysis[...] * stiff, synthesis[...], (((0,), (0,)), ((), ())),
        preferred_element_type=F32, precision=highest,
    )
    split_columns(bend_v, bend)
    own = own_s[...]
    own_v[1, :, :POINTS] = dot(own[:, :POINTS], bend, highest)
    split_columns(up_v, upsample[...])
    own_v[0] = own
    weight[...] = jnp.ones((8, RW), F32)
    weight[4:8, :RAISED] = jnp.broadcast_to(weight_s[...][None, :] * (1.0 / math.sqrt(RAISED)), (4, RAISED))
    ones = jnp.ones((3, PW), F32)
    for c in range(CELLS):
        t = own[4 * c : 4 * c + 3, :]
        norm = jnp.sum(t * t, axis=0, keepdims=True) + smooth_sq
        t1, t2, t3 = split3(t)
        s1, s2, s3 = split3(norm)
        forms = []
        for kind in range(2):
            at_row = 4 * kind
            scale = 1.0 if kind else -2.0
            rows_s[...] = jnp.zeros((LANES, PW), F32)
            for block, part in enumerate((t1, t1, t2, t2, t1, t3)):
                rows_s[8 * block + at_row : 8 * block + at_row + 3, :] = part * scale
            for block in (6, 7, 8):
                rows_s[8 * block + at_row : 8 * block + at_row + 3, :] = -ones if kind else ones
            if not kind:
                rows_s[72:73, :] = s1
                rows_s[73:74, :] = s2
                rows_s[74:75, :] = s3
            forms.append(jnp.transpose(rows_s[...]))
        for q in range(CHUNKS):
            rows = slice(q * CHUNK, (q + 1) * CHUNK)
            target[c, q] = jnp.concatenate([forms[0][rows], forms[1][rows]], axis=0).astype(BF16)

    for n in others:
        when_inside(26 - n, lambda n=n: to(n).wait_recv())

    for ref, k in ((near_s, 0), (code_s, 1), (far_s, 2)):
        ref[...] = jnp.full((LANES, LANES), -1.0, F32)
        for n in range(27):
            ref[n : n + 1, :] = halo[4 * n + k, 7:8, :]
        ref[27:28, :] = halo[4 * OWN + k, 7:8, :]
    place = lax.broadcasted_iota(jnp.int32, (32, LANES), 0)
    place_f = place.astype(F32)
    lane32 = lax.broadcasted_iota(jnp.int32, (32, LANES), 1)
    code, near, far = code_s[:32, :], near_s[:32, :], far_s[:32, :]
    mask = jnp.logical_or(
        jnp.logical_and(place < 27, code == 26.0 - place_f),
        jnp.logical_and(place == 27, code >= 0.0),
    )
    mask = jnp.logical_and(mask, jnp.logical_and(lane32 >= 64, lane32 < 64 + SLOTS))
    value = jnp.where(
        place == 27, near * 128.0 + (code * 4.0 + far), far * 128.0 + (place_f * 4.0 + near)
    )
    taken = mask.astype(F32)
    upper = (
        lax.broadcasted_iota(jnp.int32, (LANES, LANES), 0)
        < lax.broadcasted_iota(jnp.int32, (LANES, LANES), 1)
    ).astype(F32)
    lower = (
        lax.broadcasted_iota(jnp.int32, (32, 32), 1) < lax.broadcasted_iota(jnp.int32, (32, 32), 0)
    ).astype(F32)
    per_row = jnp.broadcast_to(jnp.sum(taken, axis=1, keepdims=True), (32, LANES))
    before = jnp.dot(taken, upper, preferred_element_type=F32)
    above = jnp.dot(lower, per_row, preferred_element_type=F32)
    code_s[:32, :] = jnp.where(mask, before + above, -1.0)
    near_s[:32, :] = value
    spot = jnp.transpose(code_s[...])[64 : 64 + SLOTS]
    value = jnp.transpose(near_s[...])[64 : 64 + SLOTS]
    index = lax.broadcasted_iota(jnp.int32, (SLOTS, LIST), 1).astype(F32)
    listed = jnp.zeros((SLOTS, LIST), F32)
    for n in range(28):
        listed = listed + jnp.where(spot[:, n : n + 1] == index, value[:, n : n + 1], 0.0)
    table[0:1, :] = jnp.sum(listed, axis=0, keepdims=True).astype(jnp.int32)
    total = jnp.sum(jnp.sum(taken, axis=1, keepdims=True), axis=0, keepdims=True)
    table[1:2, :] = jnp.broadcast_to(total, (1, LIST)).astype(jnp.int32)

    for n in others:
        when_inside(n, lambda n=n: to(n).wait_send())


def sums_kernel(
    table, halo, target, own, bend, up, weight,
    velocity,
    source_s, raised_s, wide0, wide1, forms0, forms1, total_s, operand_s,
):
    wide_s, forms_s = (wide0, wide1), (forms0, forms1)
    total_s[...] = jnp.zeros(total_s.shape, F32)
    source_s[...] = jnp.zeros(source_s.shape, F32)
    count = table[1, 0]
    row8 = lax.broadcasted_iota(jnp.int32, (8, RW), 0)

    def group(g, carry):
        first = g * GROUP
        last = jnp.minimum(first + GROUP, count)

        for e in range(GROUP):
            tile = halo[table[0, first + e] % 128]
            at_row = e % 2 * 4
            source_s[e // 2, at_row : at_row + 3, :LANES] = tile[0:3]
            source_s[e // 2, at_row : at_row + 3, LANES : 2 * LANES] = tile[3:6]
            source_s[e // 2, at_row : at_row + 1, 2 * LANES :] = tile[6:7]
            source_s[e // 2, at_row + 1 : at_row + 2, 2 * LANES :] = pltpu.roll(tile[6:7], 64, 1)
            source_s[e // 2, at_row + 2 : at_row + 3, 2 * LANES :] = tile[7:8]
        places = split_rows(source_s[...].reshape(GROUP * 4, PW))
        bent = split_rows(split_dot(places, bend))
        raised = split_dot(jnp.concatenate([places, bent], axis=0), up)
        raised_s[...] = raised.reshape(2, GROUP // 2, 8, RW)

        def prepare(block, odd, slot):
            block = jnp.minimum(block, GROUP // 2 - 1)
            places, forces = raised_s[0, block], raised_s[1, block]
            if odd:
                places = pltpu.roll(places, 4, 0)
            else:
                forces = pltpu.roll(forces, 4, 0)
            both = jnp.where(row8 < 4, places, forces) * weight[...]
            for c in range(3):
                wide_s[slot][c] = jnp.broadcast_to(both[c : c + 1, :], (8, RW))
                wide_s[slot][3 + c] = jnp.broadcast_to(both[4 + c : 5 + c, :], (8, RW))
            p1, p2, p3 = split3(both)
            m1, m2, m3 = split3(both * jnp.where(row8 < 4, both, pltpu.roll(both, 4, 0)))
            operand_s[...] = jnp.concatenate(
                [p1, p2, p1, p2, p3, p1, m1, m2, m3, jnp.ones((8, RW), F32)], axis=0
            ).astype(BF16)

        def cell_of(e):
            return table[0, first + e] // 128

        def expand(cell, slot, q):
            forms_s[slot][q] = dot(target[cell, q][:, :DEPTH], operand_s[...])

        def fold(cell, slot, q, begin, size):
            acc = [None] * size
            for k in range(RW // LANES):
                ln = slice(k * LANES, (k + 1) * LANES)
                ys = [wide_s[slot][c, :, ln] for c in range(3)]
                gs = [wide_s[slot][3 + c, :, ln] for c in range(3)]
                for r in range(size):
                    row = 8 * (begin + r)
                    inverse = lax.rsqrt(forms_s[slot][q, row : row + 8, ln])
                    along = forms_s[slot][q, CHUNK + row : CHUNK + row + 8, ln]
                    factor = along * inverse * (inverse * inverse)
                    new = [gs[c] * inverse - ys[c] * factor for c in range(3)] + [factor]
                    acc[r] = new if k == 0 else [a + b for a, b in zip(acc[r], new)]
            for r in range(size):
                row = 8 * (begin + r)
                for c in range(4):
                    total_s[cell, c, q, row : row + 8, :] += acc[r][c]

        def two(i, carry):
            for half in range(2):
                e = 2 * i + half
                cell = cell_of(e)
                turns = jnp.where(e < last - first, CHUNKS, 0) if half else CHUNKS
                later = cell_of(e + 1)
                prepare(i + half, 1 - half, 1 - half)

                def chunk(q, carry):
                    expand(later, 1 - half, q)
                    for begin in range(0, CHUNK // 8, 3):
                        fold(cell, half, q, begin, min(3, CHUNK // 8 - begin))
                    return carry

                lax.fori_loop(0, turns, chunk, 0)
            return carry

        prepare(0, 0, 0)
        for q in range(CHUNKS):
            expand(cell_of(0), 0, q)
        lax.fori_loop(0, (last - first + 1) // 2, two, 0)
        return carry

    lax.fori_loop(0, (count + GROUP - 1) // GROUP, group, 0)

    ones = jnp.ones((8, 2 * LANES), BF16)
    for c in range(CELLS):
        split = jnp.concatenate(split2(total_s[c].reshape(4 * POINTS, LANES)), axis=1)
        summed = dot_nt(ones, split)[0:1, :]
        parts = [summed[:, k * POINTS : (k + 1) * POINTS] for k in range(4)]
        for k in range(3):
            row = 4 * c + k
            velocity[k, c : c + 1, :] = (
                0.25 * own[1, row : row + 1, :POINTS]
                + parts[k]
                + own[0, row : row + 1, :POINTS] * parts[3]
            )


HBM = pl.BlockSpec(memory_space=pltpu.HBM)
VMEM = pl.BlockSpec(memory_space=pltpu.VMEM)
SMEM = pl.BlockSpec(memory_space=pltpu.SMEM)

HANDED = (
    ((27 * CELLS, 8, LANES), F32),
    ((2, LIST), jnp.int32),
    ((CELLS, CHUNKS, 2 * CHUNK, LANES), BF16),
    ((2, 16, PW), F32),
    ((768, PW), BF16),
    ((768, RW), BF16),
    ((8, RW), F32),
)


def sums(halo, table, target, own, bend, up, weight):
    return pl.pallas_call(
        sums_kernel,
        out_shape=jax.ShapeDtypeStruct((3, CELLS, POINTS), F32),
        in_specs=[SMEM] + [VMEM] * 6,
        out_specs=VMEM,
        scratch_shapes=[
            pltpu.VMEM((GROUP // 2, 8, PW), F32),
            pltpu.VMEM((2, GROUP // 2, 8, RW), F32),
            pltpu.VMEM((6, 8, RW), F32),
            pltpu.VMEM((6, 8, RW), F32),
            pltpu.VMEM((CHUNKS, 2 * CHUNK, RW), F32),
            pltpu.VMEM((CHUNKS, 2 * CHUNK, RW), F32),
            pltpu.VMEM((CELLS, 4, CHUNKS, CHUNK, LANES), F32),
            pltpu.VMEM((DEPTH, RW), BF16),
        ],
        compiler_params=pltpu.CompilerParams(vmem_limit_bytes=VMEM_BYTES),
        name="sums",
    )(table, halo, target, own, bend, up, weight)


def shards(surface, synthesis, analysis, stiffness, upsample, quad_weight, near_pairs, pair_count):
    outs = pl.pallas_call(
        exchange_kernel,
        out_shape=[jax.ShapeDtypeStruct(*h) for h in HANDED],
        in_specs=[HBM] * 8,
        out_specs=[VMEM] * 7,
        scratch_shapes=[
            pltpu.VMEM((LANES, LANES), F32),
            pltpu.VMEM((LANES, LANES), F32),
            pltpu.VMEM((LANES, LANES), F32),
            pltpu.VMEM((LANES, PW), F32),
            pltpu.VMEM((16, PW), F32),
            pltpu.VMEM((1, LANES), F32),
            pltpu.VMEM((3, CELLS, POINTS), F32),
            pltpu.VMEM((1, 1, 3, 1, SLOTS), jnp.int32),
            pltpu.VMEM((MODES, POINTS), F32),
            pltpu.VMEM((MODES, POINTS), F32),
            pltpu.VMEM((1, MODES), F32),
            pltpu.VMEM((POINTS, RAISED), F32),
            pltpu.VMEM((RAISED,), F32),
            pltpu.SMEM((1, 1, 1), jnp.int32),
            pltpu.SemaphoreType.DMA((8,)),
            pltpu.SemaphoreType.DMA((27,)),
            pltpu.SemaphoreType.DMA((27,)),
        ],
        compiler_params=pltpu.CompilerParams(
            collective_id=0, has_side_effects=True, vmem_limit_bytes=VMEM_BYTES
        ),
        name="exchange",
    )(pair_count, *[
        pltpu.with_memory_space_constraint(x, pltpu.HBM)
        for x in (
            jnp.swapaxes(surface[0, 0, 0], 0, 1),
            near_pairs.transpose(0, 1, 4, 2, 3), synthesis.T, analysis, stiffness[None, :],
            upsample.T, quad_weight,
        )
    ])
    velocity = sums(*outs)
    return jnp.swapaxes(velocity, 0, 1)[None, None, None]


def solution(mesh):
    return jax.shard_map(
        shards,
        mesh=mesh,
        in_specs=(
            P("tx", "ty", "tz", None, None, None),
            P(),
            P(),
            P(),
            P(),
            P(),
            P("tx", "ty", "tz", None, None),
            P("tx", "ty", "tz"),
        ),
        out_specs=P("tx", "ty", "tz", None, None, None),
        check_vma=False,
    )
```
